128 devices in a mesh: seqhi: 4 (over y), seqlo: 32 (over z, x, core).
Axes of the slice: x: 4, y: 4, z: 4, core: 2. Of those that a mesh axis runs over, the one named last changes fastest.
Arguments:
- query: bfloat16 [32768, 1280], P(('seqhi', 'seqlo')), may hold values from -6 to 6
- key: bfloat16 [32768, 1280], P(('seqhi', 'seqlo')), may hold values from -6 to 6
- value: bfloat16 [32768, 1280], P(('seqhi', 'seqlo')), may hold values from -6 to 6
- grad_out: bfloat16 [32768, 1280], P(('seqhi', 'seqlo')), may hold values from -6 to 6
- offsets: int32 [3, 10], replicated, may hold values from 0 to 63, as said below
Outputs:
- attended: bfloat16 [32768, 1280], P(('seqhi', 'seqlo'))
- grad_query: bfloat16 [32768, 1280], P(('seqhi', 'seqlo'))
- grad_key: bfloat16 [32768, 1280], P(('seqhi', 'seqlo'))
- grad_value: bfloat16 [32768, 1280], P(('seqhi', 'seqlo'))
The draws below stay inside these ranges and needn't reach their ends.
Inputs may be any that keep to these rules, and one draw needn't show every extreme that they name: offsets[l, h] is below 2^(3 * l); at every level some head has offset 2^(3 * l) - 1.
All inputs are finite; a program needn't handle non-finite values.
Results may differ from the reference program's by a relative error of at most 0.0096.
Values may be sent and summed in bfloat16 or wider, within the bound.
No kernel may reach another device: no remote copies, remote signals or barrier semaphores. Data moves between devices by JAX's collectives and lax.ppermute only.
A program may use at most 192 MiB of HBM per device.

```python
import jax
import jax.numpy as jnp

H = 10
HD = 128
SEG0 = 1024
SKIP = 3
LEVELS = 3
D = 1280
TOKENS = 32768


def draw_query(key, part):
    key = jax.random.fold_in(key, 1)
    base = jnp.clip(jax.random.normal(key, (TOKENS, H * HD), jnp.float32), -6.0, 6.0)
    return base.astype(jnp.bfloat16)


def draw_key(key, part):
    key = jax.random.fold_in(key, 2)
    base = jnp.clip(jax.random.normal(key, (TOKENS, H * HD), jnp.float32), -6.0, 6.0)
    return base.astype(jnp.bfloat16)


def draw_offsets(key, part):
    key = jax.random.fold_in(key, 5)
    table = []
    for level_id in range(LEVELS):
        stride = 2 ** (SKIP * level_id)
        drawn = jax.random.randint(jax.random.fold_in(key, level_id), (H,), 0, stride)
        chosen = jax.random.randint(jax.random.fold_in(key, 100 + level_id), (), 0, H)
        drawn = jnp.where(jnp.arange(H) == chosen, stride - 1, drawn)
        table.append(drawn)
    return jnp.stack(table).astype(jnp.int32)


def block_scale(key, dims, pieces, smallest, largest):
    gain = 1.0
    for dim, blocks in pieces:
        steps = jax.random.uniform(jax.random.fold_in(jax.random.fold_in(key, 6), dim), (blocks,), jnp.float32, smallest / len(pieces), largest / len(pieces))
        gain = gain * jnp.repeat(jnp.exp(steps), dims[dim] // blocks).reshape((-1,) + (1,) * (len(dims) - 1 - dim))
    return gain


def normal_values(own_key, shape, scale, reach, shards=(), held_as=jnp.bfloat16):
    values = scale * jax.random.normal(own_key, shape, jnp.float32)
    if shards:
        values = values * block_scale(own_key, shape, shards, -0.22, 0.18)
    return jnp.clip(values, -reach, reach).astype(held_as)


def setup_inputs(seed: int = 0) -> dict:
    keys = jax.random.split(jax.random.key(seed), 6)
    query = draw_query(jax.random.fold_in(keys[5], 71), 0)
    key = draw_key(jax.random.fold_in(keys[5], 71), 0)
    value = normal_values(keys[2], (TOKENS, D), 1.0, 6.0, ((0, 128),))
    grad_out = normal_values(keys[3], (TOKENS, D), 1.0, 6.0, ((0, 128),))
    offsets = draw_offsets(jax.random.fold_in(keys[5], 71), 0)
    return dict(query=query, key=key, value=value, grad_out=grad_out, offsets=offsets)


def pick(source, shifts, stride):
    row_count = source.shape[0]
    grouped = source.reshape((row_count // stride, stride) + source.shape[1:])
    chosen = jnp.arange(stride)[:, None] == shifts[None, :]
    chosen = chosen.reshape((1, stride, shifts.shape[0]) + (1,) * (source.ndim - 2))
    picked = jnp.sum(jnp.where(chosen, grouped, jnp.zeros((), source.dtype)), axis=1)
    return jnp.moveaxis(picked, 1, 0)


def spread(values, shifts, stride, filler):
    lifted = jnp.moveaxis(values, 0, 1)
    count_rows = lifted.shape[0]
    chosen = jnp.arange(stride)[:, None] == shifts[None, :]
    chosen = chosen.reshape((1, stride, shifts.shape[0]) + (1,) * (lifted.ndim - 2))
    placed = jnp.where(chosen, lifted[:, None], filler)
    return placed.reshape((count_rows * stride,) + lifted.shape[1:])


def scores_of(sel_query, sel_key, scaling):
    return jnp.einsum("hsid,hsjd->hsij", sel_query.astype(jnp.float32), sel_key.astype(jnp.float32)) * scaling


def reference(query, key, value, grad_out, offsets):
    scaling = HD ** -0.5
    query3 = query.reshape(TOKENS, H, HD)
    key3 = key.reshape(TOKENS, H, HD)
    value3 = value.reshape(TOKENS, H, HD)
    grad3 = grad_out.reshape(TOKENS, H, HD)
    levels = []
    for level_id in range(LEVELS):
        stride = 2 ** (SKIP * level_id)
        segment = min(SEG0 * stride, TOKENS)
        shape4 = (H, TOKENS // segment, segment // stride, HD)
        shifts = offsets[level_id]
        levels.append((stride, shifts, pick(query3, shifts, stride).reshape(shape4), pick(key3, shifts, stride).reshape(shape4), pick(value3, shifts, stride).reshape(shape4), pick(grad3, shifts, stride).reshape(shape4)))
    peak_score = jnp.full((TOKENS, H), -jnp.inf, jnp.float32)
    for stride, shifts, sel_query, sel_key, sel_value, sel_grad in levels:
        scores = scores_of(sel_query, sel_key, scaling)
        peak_score = jnp.maximum(peak_score, spread(jnp.max(scores, -1).reshape(H, -1), shifts, stride, -jnp.inf))
    total_exp = jnp.zeros((TOKENS, H), jnp.float32)
    for stride, shifts, sel_query, sel_key, sel_value, sel_grad in levels:
        scores = scores_of(sel_query, sel_key, scaling)
        peak_sel = pick(peak_score, shifts, stride).reshape(scores.shape[:3])
        total_exp = total_exp + spread(jnp.sum(jnp.exp(scores - peak_sel[..., None]), -1).reshape(H, -1), shifts, stride, 0.0)
    log_total = peak_score + jnp.log(total_exp)
    full_out = jnp.zeros((TOKENS, H, HD), jnp.float32)
    for stride, shifts, sel_query, sel_key, sel_value, sel_grad in levels:
        scores = scores_of(sel_query, sel_key, scaling)
        log_sel = pick(log_total, shifts, stride).reshape(scores.shape[:3])
        prob_b = jnp.exp(scores - log_sel[..., None]).astype(jnp.bfloat16)
        partial_value = jnp.einsum("hsij,hsjd->hsid", prob_b.astype(jnp.float32), sel_value.astype(jnp.float32))
        full_out = full_out + spread(partial_value.reshape(H, -1, HD), shifts, stride, 0.0)
    row_dot = jnp.sum(grad3.astype(jnp.float32) * full_out, -1)
    grad_query = jnp.zeros((TOKENS, H, HD), jnp.float32)
    grad_key = jnp.zeros((TOKENS, H, HD), jnp.float32)
    grad_value = jnp.zeros((TOKENS, H, HD), jnp.float32)
    for stride, shifts, sel_query, sel_key, sel_value, sel_grad in levels:
        scores = scores_of(sel_query, sel_key, scaling)
        log_sel = pick(log_total, shifts, stride).reshape(scores.shape[:3])
        dot_sel = pick(row_dot, shifts, stride).reshape(scores.shape[:3])
        prob = jnp.exp(scores - log_sel[..., None])
        prob_b = prob.astype(jnp.bfloat16)
        dprob = jnp.einsum("hsid,hsjd->hsij", sel_grad.astype(jnp.float32), sel_value.astype(jnp.float32))
        dscore = (prob * (dprob - dot_sel[..., None])).astype(jnp.bfloat16).astype(jnp.float32)
        query_part = jnp.einsum("hsij,hsjd->hsid", dscore, sel_key.astype(jnp.float32)) * scaling
        key_part = jnp.einsum("hsij,hsid->hsjd", dscore, sel_query.astype(jnp.float32)) * scaling
        value_part = jnp.einsum("hsij,hsid->hsjd", prob_b.astype(jnp.float32), sel_grad.astype(jnp.float32))
        grad_query = grad_query + spread(query_part.reshape(H, -1, HD), shifts, stride, 0.0)
        grad_key = grad_key + spread(key_part.reshape(H, -1, HD), shifts, stride, 0.0)
        grad_value = grad_value + spread(value_part.reshape(H, -1, HD), shifts, stride, 0.0)
    return (full_out.reshape(TOKENS, H * HD).astype(jnp.bfloat16), grad_query.reshape(TOKENS, H * HD).astype(jnp.bfloat16), grad_key.reshape(TOKENS, H * HD).astype(jnp.bfloat16), grad_value.reshape(TOKENS, H * HD).astype(jnp.bfloat16))
```

```python
import functools

import jax
import jax.numpy as jnp
from jax import lax
from jax.experimental import pallas as pl
from jax.experimental.pallas import tpu as pltpu
from jax.sharding import PartitionSpec as P

H = 10
HD = 128
ROWS = 256
LOG2E = 1.4426950408889634
SCALING = HD ** -0.5
NEG = -1e30
VMEM_LIMIT = 48 * 1024 * 1024


def swapped(x, axis, mask):
    return lax.ppermute(x, axis, [(i, i ^ mask) for i in range(lax.axis_size(axis))])


def after(x, *others):
    return lax.optimization_barrier((x,) + others)[0]


def dot_nt(a, b):
    return lax.dot_general(a, b, (((1,), (1,)), ((), ())), preferred_element_type=jnp.float32)


def dot_nn(a, b):
    return lax.dot_general(a, b, (((1,), (0,)), ((), ())), preferred_element_type=jnp.float32)


def pick_kernel(off_ref, k_ref, v_ref, q_ref, g_ref, one_ref, two_ref):
    h = pl.program_id(0)
    i = lax.broadcasted_iota(jnp.int32, (48, ROWS), 0)
    p = lax.broadcasted_iota(jnp.int32, (48, ROWS), 1)
    target = jnp.where(i < 32, 8 * i + off_ref[1, h], 64 * (i - 32) + off_ref[2, h])
    onehot = (p == target).astype(jnp.bfloat16)
    for t, ref in enumerate((k_ref, v_ref, q_ref, g_ref)):
        rows = dot_nn(onehot, ref[...]).astype(jnp.bfloat16)
        one_ref[t] = rows[:32]
        two_ref[t] = rows[32:]


def pick(key, value, query, grad_out, offsets):
    column = pl.BlockSpec((ROWS, HD), lambda h, off: (0, h))
    return pl.pallas_call(
        pick_kernel,
        grid_spec=pltpu.PrefetchScalarGridSpec(
            num_scalar_prefetch=1,
            grid=(H,),
            in_specs=[column] * 4,
            out_specs=[
                pl.BlockSpec((4, 32, HD), lambda h, off: (0, 0, h)),
                pl.BlockSpec((4, 16, HD), lambda h, off: (0, 0, h)),
            ],
        ),
        out_shape=[
            jax.ShapeDtypeStruct((4, 32, H * HD), jnp.bfloat16),
            jax.ShapeDtypeStruct((4, 16, H * HD), jnp.bfloat16),
        ],
        cost_estimate=pl.CostEstimate(flops=2 * 48 * 256 * 128 * 40, bytes_accessed=3_400_000, transcendentals=0),
        name="pick_rows",
    )(offsets, key, value, query, grad_out)


def level_masks(off_ref, h):
    row = lax.broadcasted_iota(jnp.int32, (ROWS, 1), 0)
    return ((row & 7) == off_ref[1, h], (row & 63) == off_ref[2, h])


def forward_kernel(off_ref, q_ref, g_ref, *refs):
    k_refs, v_refs, (att_ref, dq_ref, stat_ref) = refs[:8], refs[8:16], refs[16:]
    h = pl.program_id(0)
    sel1, sel2 = level_masks(off_ref, h)
    masks = [None] * 4 + [sel1] * 2 + [sel2] * 2
    q = q_ref[...]
    g = g_ref[...]
    keys = [r[...].reshape(-1, HD) for r in k_refs]
    values = [r[...].reshape(-1, HD) for r in v_refs]
    scores = []
    for k, mask in zip(keys, masks):
        s = dot_nt(q, k) * (SCALING * LOG2E)
        scores.append(s if mask is None else jnp.where(mask, s, NEG))
    peak = functools.reduce(jnp.maximum, [jnp.max(s, 1, keepdims=True) for s in scores])
    exps = [jnp.exp2(s - peak) for s in scores]
    total = sum(jnp.sum(e, 1, keepdims=True) for e in exps)
    inv = 1.0 / total
    probs = [e * inv for e in exps]
    out = sum(dot_nn(p.astype(jnp.bfloat16), v) for p, v in zip(probs, values))
    att_ref[...] = out.astype(jnp.bfloat16)
    row_dot = jnp.sum(out * g.astype(jnp.float32), 1, keepdims=True)
    dq = jnp.zeros((ROWS, HD), jnp.float32)
    for p, k, v in zip(probs, keys, values):
        ds = (p * (dot_nt(g, v) - row_dot)).astype(jnp.bfloat16)
        dq = dq + dot_nn(ds, k)
    dq_ref[...] = (dq * SCALING).astype(jnp.bfloat16)
    lse = peak + jnp.log2(total)
    i = lax.broadcasted_iota(jnp.int32, (ROWS, 384), 0)
    j = lax.broadcasted_iota(jnp.int32, (ROWS, 384), 1)
    target = jnp.where(j < 256, j, jnp.where(j < 288, 8 * (j - 256) + off_ref[1, h], 64 * (j - 288) + off_ref[2, h]))
    hit = i == target
    stat_ref[0] = jnp.concatenate(
        [jnp.sum(jnp.where(hit, x, 0.0), 0, keepdims=True) for x in (lse, row_dot)], 0
    )


def backward_kernel(off_ref, k_ref, v_ref, *refs):
    q_refs, g_refs, s_refs, (dk_ref, dv_ref) = refs[:8], refs[8:16], refs[16:24], refs[24:]
    h = pl.program_id(0)
    sel1, sel2 = level_masks(off_ref, h)
    masks = [None] * 4 + [sel1] * 2 + [sel2] * 2
    k = k_ref[...]
    v = v_ref[...]
    dk = jnp.zeros((ROWS, HD), jnp.float32)
    dv = jnp.zeros((ROWS, HD), jnp.float32)
    for q_ref, g_ref, s_ref, mask in zip(q_refs, g_refs, s_refs, masks):
        q = q_ref[...].reshape(-1, HD)
        g = g_ref[...].reshape(-1, HD)
        lse = s_ref[0, 0:1, : q.shape[0]]
        row_dot = s_ref[0, 1:2, : q.shape[0]]
        s = dot_nt(k, q) * (SCALING * LOG2E) - lse
        if mask is not None:
            s = jnp.where(mask, s, NEG)
        p = jnp.exp2(s)
        ds = (p * (dot_nt(v, g) - row_dot)).astype(jnp.bfloat16)
        dv = dv + dot_nn(p.astype(jnp.bfloat16), g)
        dk = dk + dot_nn(ds, q)
    dk_ref[...] = (dk * SCALING).astype(jnp.bfloat16)
    dv_ref[...] = dv.astype(jnp.bfloat16)


COLUMN = pl.BlockSpec((ROWS, HD), lambda h, off: (0, h))


def one_spec(t):
    return pl.BlockSpec((4, 4, 1, 32, HD), lambda h, off: (0, 0, t, 0, h))


def two_spec(t):
    return pl.BlockSpec((4, 4, 1, 16, HD), lambda h, off: (0, 0, t, 0, h))


def stat_spec(width):
    return pl.BlockSpec((1, 2, width), lambda h, off: (h, 0, 0))


PARAMS = pltpu.CompilerParams(vmem_limit_bytes=VMEM_LIMIT)
COST = pl.CostEstimate(flops=2 * 256 * 2560 * 128 * 40, bytes_accessed=15_000_000, transcendentals=256 * 2560 * 10)


def forward(offsets, q, g, k0, v0, one, two):
    wide = jax.ShapeDtypeStruct((ROWS, H * HD), jnp.bfloat16)
    return pl.pallas_call(
        forward_kernel,
        grid_spec=pltpu.PrefetchScalarGridSpec(
            num_scalar_prefetch=1,
            grid=(H,),
            in_specs=[COLUMN] * 2
            + [COLUMN] * 4 + [one_spec(0)] * 2 + [two_spec(0)] * 2
            + [COLUMN] * 4 + [one_spec(1)] * 2 + [two_spec(1)] * 2,
            out_specs=[COLUMN, COLUMN, stat_spec(384)],
        ),
        out_shape=[wide, wide, jax.ShapeDtypeStruct((H, 2, 384), jnp.float32)],
        compiler_params=PARAMS,
        cost_estimate=COST,
        name="forward",
    )(offsets, q, g, *k0, *one, *two, *v0, *one, *two)


def backward(offsets, k, v, q0, g0, one, two, s0, s1, s2):
    wide = jax.ShapeDtypeStruct((ROWS, H * HD), jnp.bfloat16)
    return pl.pallas_call(
        backward_kernel,
        grid_spec=pltpu.PrefetchScalarGridSpec(
            num_scalar_prefetch=1,
            grid=(H,),
            in_specs=[COLUMN] * 2
            + [COLUMN] * 4 + [one_spec(0)] * 2 + [two_spec(2)] * 2
            + [COLUMN] * 4 + [one_spec(1)] * 2 + [two_spec(3)] * 2
            + [stat_spec(384)] * 4 + [stat_spec(512)] * 2 + [stat_spec(256)] * 2,
            out_specs=[COLUMN, COLUMN],
        ),
        out_shape=[wide, wide],
        compiler_params=PARAMS,
        cost_estimate=COST,
        name="backward",
    )(offsets, k, v, *q0, *one, *two, *g0, *one, *two, *s0, *s1, *s2)


CORE, XS, ZS, YS = 1, (2, 4, 6), (8, 16, 24), (1, 2, 3)


def around(x, axis, masks):
    return [x] + [swapped(x, axis, m) for m in masks]


def body(query, key, value, grad_out, offsets):
    kx = swapped(key, "seqlo", XS[0])
    one, two = pick(key, value, query, grad_out, offsets)
    two = two[:, :4]

    two = jnp.concatenate(around(two, "seqlo", XS), 1)
    two = jnp.stack(around(two, "seqlo", ZS))
    two = jnp.stack(around(two, "seqhi", YS))
    two_c = swapped(two, "seqlo", CORE)

    one_a = jnp.stack(around(one[:2], "seqlo", XS))
    one_b = jnp.stack(around(one[2:], "seqlo", XS))
    vx = swapped(after(value, one_a), "seqlo", XS[0])
    full_a = jnp.stack(around(one_a, "seqlo", ZS))
    full_b = jnp.stack(around(after(one_b, full_a), "seqlo", ZS))
    full_ac = swapped(full_a, "seqlo", CORE)
    full_bc = swapped(full_b, "seqlo", CORE)

    qx = swapped(after(query, kx), "seqlo", XS[0])
    gx = swapped(after(grad_out, vx), "seqlo", XS[0])
    kc, vc, qc, gc, kxc, vxc, qxc, gxc = [
        swapped(t, "seqlo", CORE) for t in (key, value, query, grad_out, kx, vx, qx, gx)
    ]

    attended, grad_query, stats = forward(
        offsets, query, grad_out, [key, kc, kx, kxc], [value, vc, vx, vxc], [full_a, full_ac], [two, two_c]
    )

    sx = swapped(stats, "seqlo", XS[0])
    sc = swapped(stats, "seqlo", CORE)
    sxc = swapped(sx, "seqlo", CORE)
    small = stats[:, :, 256:]
    small = jnp.stack([small, sx[:, :, 256:]] + [swapped(small, "seqlo", m) for m in XS[1:]])
    small = jnp.stack(around(small, "seqlo", ZS))
    small_c = swapped(small, "seqlo", CORE)
    tiny = small[..., 32:36].transpose(2, 3, 0, 1, 4).reshape(H * 2, 64)
    tiny = jnp.stack(around(tiny, "seqhi", YS), 1).reshape(H, 2, 256)
    tiny_c = swapped(tiny, "seqlo", CORE)
    s1 = [t[..., :32].transpose(2, 3, 0, 1, 4).reshape(H, 2, 512) for t in (small, small_c)]

    grad_key, grad_value = backward(
        offsets, key, value, [query, qc, qx, qxc], [grad_out, gc, gx, gxc],
        [full_b, full_bc], [two, two_c], [stats, sc, sx, sxc], s1, [tiny, tiny_c],
    )
    return attended, grad_query, grad_key, grad_value


def solution(mesh):
    spec = P(("seqhi", "seqlo"), None)
    return jax.shard_map(
        body,
        mesh=mesh,
        in_specs=(spec, spec, spec, spec, P()),
        out_specs=(spec, spec, spec, spec),
        check_vma=False,
    )
```

```python
import functools

import jax
import jax.numpy as jnp
from jax import lax
from jax.experimental import pallas as pl
from jax.experimental.pallas import tpu as pltpu
from jax.sharding import PartitionSpec as P

H = 10
HD = 128
ROWS = 256
SCALING = HD ** -0.5
LOG2E = 1.4426950408889634
FACTOR = SCALING * LOG2E
NEG = -1e30
WIDE = (ROWS, H * HD)
HALF = jnp.bfloat16
FULL = jnp.float32


def swapped(x, axis, mask):
    return lax.ppermute(x, axis, [(i, i ^ mask) for i in range(lax.axis_size(axis))])


def after(x, *others):
    return lax.optimization_barrier((x,) + others)[0]


def dot_nt(a, b):
    return lax.dot_general(a, b, (((1,), (1,)), ((), ())), preferred_element_type=FULL)


def dot_nn(a, b):
    return lax.dot_general(a, b, (((1,), (0,)), ((), ())), preferred_element_type=FULL)


def dot_exact(a, b):
    return lax.dot_general(
        a, b, (((1,), (0,)), ((), ())), precision=lax.Precision.HIGHEST, preferred_element_type=FULL
    )


def grid_ij(shape):
    return (
        lax.broadcasted_iota(jnp.int32, shape, 0),
        lax.broadcasted_iota(jnp.int32, shape, 1),
    )


def eye_column(row, n):
    i, j = grid_ij((n, n))
    return jnp.sum(jnp.where(i == j, row, 0.0), 1, keepdims=True)


def heads_of(step, parts=2):
    return [(step * parts + part, slice(part * HD, (part + 1) * HD)) for part in range(parts)]


def pick_kernel(off_ref, k_ref, v_ref, q_ref, g_ref, out_ref):
    step = pl.program_id(0)

    @pl.when(step < 5)
    def _():
        for h, cols in heads_of(step):
            i, p = grid_ij((32, ROWS))
            one = (p == 8 * i + off_ref[1, h]).astype(HALF)
            j, p = grid_ij((16, ROWS))
            two = p == 64 * (j & 3) + off_ref[2, h]
            sources = [r[:, cols] for r in (k_ref, v_ref, q_ref, g_ref)]
            rows = [dot_nn(one, x).astype(HALF) for x in sources]
            small = sum(
                dot_nn((two & (j // 4 == t)).astype(HALF), x) for t, x in enumerate(sources)
            )
            out_ref[0:32, cols] = rows[0]
            out_ref[32:64, cols] = rows[1]
            out_ref[64:80, cols] = small.astype(HALF)
            out_ref[80:112, cols] = rows[2]
            out_ref[112:144, cols] = rows[3]

    @pl.when(step == 5)
    def _():
        out_ref[...] = jnp.zeros(out_ref.shape, HALF)


def softmax_all(problems):
    scores = [[dot_nt(q, k) * FACTOR for k in keys] for q, keys, _ in problems]
    peaks = [
        functools.reduce(jnp.maximum, [jnp.max(s, 1, keepdims=True) for s in part])
        for part in scores
    ]
    exps = [[jnp.exp2(s - peak) for s in part] for part, peak in zip(scores, peaks)]
    totals = [sum(jnp.sum(e, 1, keepdims=True) for e in part) for part in exps]
    outs = [
        sum(dot_nn(e.astype(HALF), v) for e, v in zip(part, values))
        for part, (_, _, values) in zip(exps, problems)
    ]
    return peaks, totals, outs


def lanes_of(columns):
    _, j = grid_ij((columns[0].shape[0], 128))
    block = jnp.zeros((columns[0].shape[0], 128), FULL)
    for lane, column in enumerate(columns):
        block = jnp.where(j == lane, column, block)
    return block


def near_kernel(q_ref, *refs):
    k_refs, v_refs, (out_ref, stat_ref) = refs[:4], refs[4:8], refs[8:]
    parts = heads_of(0)
    peaks, totals, outs = softmax_all(
        [(q_ref[:, c], [k[:, c] for k in k_refs], [v[:, c] for v in v_refs]) for _, c in parts]
    )
    for (_, c), out, total in zip(parts, outs, totals):
        out_ref[:, c] = out * (1.0 / total)
    stat_ref[0] = lanes_of([peak + jnp.log2(total) for peak, total in zip(peaks, totals)])


def group_rows(a_ref, b_ref, y_ref, c):
    one = {
        "k": a_ref[0, :, 0:32, c], "v": a_ref[0, :, 32:64, c],
        "q": b_ref[0, :, 0:32, c], "g": b_ref[0, :, 32:64, c],
    }
    one = {name: x.reshape(128, HD) for name, x in one.items()}
    two = {name: y_ref[0, t, 0:16, c] for t, name in enumerate("kvqg")}
    return one, two


def group_forward_kernel(zs_ref, a0_ref, a1_ref, y0_ref, y1_ref, ret_ref):
    problems = []
    parts = heads_of(0, 3)
    for _, c in parts:
        q1 = zs_ref[:, 80:112, c].reshape(128, HD)
        problems.append((
            q1,
            [r[:, :, 0:32, c].reshape(512, HD) for r in (a0_ref, a1_ref)],
            [r[:, :, 32:64, c].reshape(512, HD) for r in (a0_ref, a1_ref)],
        ))
        problems.append((
            y0_ref[0, 2, 0:16, c],
            [r[:, 0, :, c].reshape(256, HD) for r in (y0_ref, y1_ref)],
            [r[:, 1, :, c].reshape(256, HD) for r in (y0_ref, y1_ref)],
        ))
    peaks, totals, outs = softmax_all(problems)
    outs = [out * (1.0 / total) for out, total in zip(outs, totals)]
    lses = [peak + jnp.log2(total) for peak, total in zip(peaks, totals)]
    one, two = lanes_of(lses[0::2]), lanes_of(lses[1::2])
    for m in range(4):
        for (_, c), out1, out2 in zip(parts, outs[0::2], outs[1::2]):
            ret_ref[m, 0:32, c] = out1[32 * m : 32 * m + 32]
            ret_ref[m, 32:36, c] = out2[4 * m : 4 * m + 4]
        ret_ref[m, 0:32, 384:512] = one[32 * m : 32 * m + 32]
        ret_ref[m, 32:36, 384:512] = two[4 * m : 4 * m + 4]
        ret_ref[m, 36:40, :] = jnp.zeros((4, 512), FULL)


def merge_kernel(off_ref, z_ref, near_ref, near_stat_ref, g_ref, *refs):
    o_refs, l_refs, (att_ref, stat_ref, row_ref, sel_ref) = refs[:2], refs[2:4], refs[4:]
    step = pl.program_id(0)
    lses, dots = [], []
    for part, (h, c) in enumerate(heads_of(step)):
        p, i = grid_ij((ROWS, 40))
        hit1 = (p == 8 * i + off_ref[1, h]) & (i < 32)
        hit2 = (p == 64 * (i - 32) + off_ref[2, h]) & (i >= 32) & (i < 36)
        p, _ = grid_ij((ROWS, 1))
        chosen1 = (p & 7) == off_ref[1, h]
        chosen2 = (p & 63) == off_ref[2, h]
        _, j = grid_ij((40, 128))
        lse12 = jnp.where(j == h % 3, l_refs[part][0], 0.0)
        both = dot_exact(jnp.concatenate([hit1, hit2], 0).astype(FULL), lse12)
        both = jnp.sum(both, 1, keepdims=True)
        lse0 = near_stat_ref[0, :, part : part + 1]
        lse1 = jnp.where(chosen1, both[:ROWS], NEG)
        lse2 = jnp.where(chosen2, both[ROWS:], NEG)
        peak = jnp.maximum(jnp.maximum(lse0, lse1), lse2)
        w0, w1, w2 = [jnp.exp2(x - peak) for x in (lse0, lse1, lse2)]
        total = w0 + w1 + w2
        out12 = o_refs[part][0]
        high = out12.astype(HALF)
        low = (out12 - high.astype(FULL)).astype(HALF)
        pieces = jnp.concatenate([high, low], 1)
        up1 = dot_nn(hit1.astype(HALF), pieces)
        up2 = dot_nn(hit2.astype(HALF), pieces)
        out = near_ref[:, c] * w0 + (up1[:, :HD] + up1[:, HD:]) * w1 + (up2[:, :HD] + up2[:, HD:]) * w2
        out = out * (1.0 / total)
        att_ref[:, c] = out.astype(HALF)
        lses.append(peak + jnp.log2(total))
        dots.append(jnp.sum(out * g_ref[:, c].astype(FULL), 1, keepdims=True))
    block = lanes_of(lses + dots)
    stat_ref[0] = block
    row_ref[0] = block.T[0:8]
    for part, (h, c) in enumerate(heads_of(step)):
        p, j = grid_ij((ROWS, 128))
        target = jnp.where(j < 32, 8 * j + off_ref[1, h], 64 * (j - 32) + off_ref[2, h])
        hit = (p == target) & (j < 36)
        sel_ref[part] = jnp.concatenate(
            [jnp.sum(jnp.where(hit, x[part], 0.0), 0, keepdims=True) for x in (lses, dots)], 0
        )


def gradients(problems):
    probs = [jnp.exp2(dot_nt(a, b) * FACTOR - lse) for a, b, _, _, lse, _ in problems]
    dprobs = [dot_nt(c, d) for _, _, c, d, _, _ in problems]
    return [
        (prob.astype(HALF), (prob * (dprob - row_dot)).astype(HALF))
        for prob, dprob, (_, _, _, _, _, row_dot) in zip(probs, dprobs, problems)
    ]


def near_query_kernel(q_ref, g_ref, stat_ref, *refs):
    k_refs, v_refs, (dq_ref,) = refs[:4], refs[4:8], refs[8:]
    problems = []
    for part, (_, c) in enumerate(heads_of(0)):
        lse = stat_ref[0, :, part : part + 1]
        row_dot = stat_ref[0, :, part + 2 : part + 3]
        for k, v in zip(k_refs, v_refs):
            problems.append((q_ref[:, c], k[:, c], g_ref[:, c], v[:, c], lse, row_dot))
    done = gradients(problems)
    for part, (_, c) in enumerate(heads_of(0)):
        dq_ref[:, c] = sum(dot_nn(ds, k[:, c]) for (_, ds), k in zip(done[4 * part :], k_refs))


def group_backward_kernel(a0_ref, a1_ref, b0_ref, b1_ref, y0_ref, y1_ref, s10, s11, s20, s21, out_ref):
    problems, others = [], []
    parts = heads_of(0, 3)
    for j, c in parts:
        one, two = group_rows(a0_ref, b0_ref, y0_ref, c)
        sides = []
        for a, b, s in ((a0_ref, b0_ref, s10), (a1_ref, b1_ref, s11)):
            sides.append((
                a[:, :, 0:32, c].reshape(512, HD), a[:, :, 32:64, c].reshape(512, HD),
                b[:, :, 0:32, c].reshape(512, HD), b[:, :, 32:64, c].reshape(512, HD),
                s[j, 0:1, :], s[j, 1:2, :],
            ))
        for y, s in ((y0_ref, s20), (y1_ref, s21)):
            sides.append(tuple(y[:, t, :, c].reshape(256, HD) for t in range(4)) + (s[j, 0:1, :], s[j, 1:2, :]))
        own = (one, one, two, two)
        for rows, n, (k, v, q, g, lse, row_dot) in zip(own, (128, 128, 16, 16), sides):
            first = sides[0] if n == 128 else sides[2]
            lse_own = eye_column(first[4][:, :n], n)
            dot_own = eye_column(first[5][:, :n], n)
            problems.append((rows["q"], k, rows["g"], v, lse_own, dot_own))
            others.append(k)
            problems.append((rows["k"], q, rows["v"], g, lse, row_dot))
            others.append((q, g))
    done = gradients(problems)
    for j, c in parts:
        mine, rest = done[8 * j : 8 * j + 8], others[8 * j : 8 * j + 8]
        dq = [dot_nn(mine[n][1], rest[n]) * SCALING for n in (0, 2, 4, 6)]
        dk = [dot_nn(mine[n][1], rest[n][0]) * SCALING for n in (1, 3, 5, 7)]
        dv = [dot_nn(mine[n][0], rest[n][1]) for n in (1, 3, 5, 7)]
        one = [(x[0] + x[1]).astype(HALF) for x in (dq, dk, dv)]
        two = [x[2] + x[3] for x in (dq, dk, dv)]
        for m in range(4):
            for t in range(3):
                out_ref[m, 32 * t : 32 * t + 32, c] = one[t][32 * m : 32 * m + 32]
            small = [x[4 * m : 4 * m + 4] for x in two] + [jnp.zeros((4, HD), FULL)]
            out_ref[m, 96:112, c] = jnp.concatenate(small, 0).astype(HALF)


def final_kernel(off_ref, z_ref, k_ref, v_ref, dq_near_ref, *refs):
    q_refs, g_refs, s_refs = refs[:4], refs[4:8], refs[8:12]
    r_refs, (dq_ref, dk_ref, dv_ref) = refs[12:14], refs[14:]
    step = pl.program_id(0)
    problems = []
    for part, (_, c) in enumerate(heads_of(0)):
        for q, g, s in zip(q_refs, g_refs, s_refs):
            lse, row_dot = s[0, part : part + 1, :], s[0, part + 2 : part + 3, :]
            problems.append((k_ref[:, c], q[:, c], v_ref[:, c], g[:, c], lse, row_dot))
    done = gradients(problems)
    for part, (h, c) in enumerate(heads_of(step)):
        lifted = []
        p, r = grid_ij((ROWS, 112))
        t1 = jnp.where(r < 96, r // 32, (r - 96) // 4)
        target = jnp.where(r < 96, 8 * (r & 31) + off_ref[1, h], 64 * (r & 3) + off_ref[2, h])
        for t in range(3):
            hit = ((t1 == t) & (p == target)).astype(HALF)
            lifted.append(dot_nn(hit, r_refs[part][0]))
        mine = done[4 * part : 4 * part + 4]
        dk = sum(dot_nn(ds, q[:, c]) for (_, ds), q in zip(mine, q_refs))
        dv = sum(dot_nn(prob, g[:, c]) for (prob, _), g in zip(mine, g_refs))
        dq_ref[:, c] = (dq_near_ref[:, c] * SCALING + lifted[0]).astype(HALF)
        dk_ref[:, c] = (dk * SCALING + lifted[1]).astype(HALF)
        dv_ref[:, c] = (dv + lifted[2]).astype(HALF)


COLUMNS = pl.BlockSpec((ROWS, 2 * HD), lambda s, *_: (0, s))
LANES = pl.BlockSpec((1, ROWS, 128), lambda s, *_: (s, 0, 0))
STAT_ROWS = pl.BlockSpec((1, 8, ROWS), lambda s, *_: (s, 0, 0))


def whole(*shape):
    return pl.BlockSpec(shape, lambda *_: (0,) * len(shape))


def returned_spec(part, rows, lane_block=None):
    def index(s, off, z):
        h = 2 * s + part
        return (h // 3) ^ z[0], 0, h % 3 if lane_block is None else lane_block

    return pl.BlockSpec((1, rows, HD), index)


def array(*shape, dtype=HALF):
    return jax.ShapeDtypeStruct(shape, dtype)


def call(kernel, name, steps, in_specs, out_specs, out_shape, operands, prefetch=0, room=48):
    return pl.pallas_call(
        kernel,
        grid_spec=pltpu.PrefetchScalarGridSpec(
            num_scalar_prefetch=prefetch, grid=(steps,), in_specs=in_specs, out_specs=out_specs
        ),
        out_shape=out_shape,
        compiler_params=pltpu.CompilerParams(vmem_limit_bytes=room * 1024 * 1024),
        cost_estimate=pl.CostEstimate(flops=100_000_000, bytes_accessed=1_000_000, transcendentals=0),
        name=name,
    )(*operands)


CORE, X1, X3 = 1, 2, 6
ZS = (8, 16, 24)


def two_steps(x, axis, first, second):
    x = jnp.stack([x, swapped(x, axis, first)])
    return jnp.concatenate([x, swapped(x, axis, second)], 0)


def around(x, axis, masks):
    return [x] + [swapped(x, axis, m) for m in masks]


def core(x):
    return swapped(x, "seqlo", CORE)


def body(query, key, value, grad_out, offsets):
    z = lax.axis_index("seqlo") // 8
    zs_index = z.reshape(1).astype(jnp.int32)
    kx = swapped(key, "seqlo", X1)
    vx = swapped(value, "seqlo", X1)
    picked = call(
        pick_kernel, "pick_rows", 6,
        [pl.BlockSpec((ROWS, 2 * HD), lambda s, *_: (0, jnp.minimum(s, 4)))] * 4,
        [pl.BlockSpec((144, 2 * HD), lambda s, *_: (0, s))],
        [array(144, 12 * HD)],
        (offsets, key, value, query, grad_out), prefetch=1, room=60,
    )[0]

    def for_z(x, m, width):
        return lax.dynamic_slice_in_dim(x, (z ^ m) * width, width, x.ndim - 1)

    zs = jnp.stack(
        [for_z(picked, 0, 384)]
        + [swapped(for_z(picked, m, 384), "seqlo", 8 * m) for m in (1, 2, 3)]
    )
    a = two_steps(zs[:, :80], "seqlo", X1, X3)
    y = a[:, :, 64:80].reshape(4, 4, 4, 4, 384).transpose(2, 0, 1, 3, 4).reshape(4, 64, 384)
    y = jnp.stack(around(y, "seqhi", (1, 2, 3)))
    b = two_steps(after(zs[:, 80:], a), "seqlo", X1, X3)
    qx = swapped(after(query, vx), "seqlo", X1)
    gx = swapped(after(grad_out, vx), "seqlo", X1)
    a1, y1, b1 = core(a), core(y), core(b)
    keys0 = [key, core(key), kx, core(kx)]
    values0 = [value, core(value), vx, core(vx)]

    near, near_stat = call(
        near_kernel, "near_forward", 5, [COLUMNS] * 9, [COLUMNS, LANES],
        [array(*WIDE, dtype=FULL), array(5, ROWS, 128, dtype=FULL)],
        (query, *keys0, *values0),
    )
    a_spec, b_spec, y_spec = whole(4, 4, 80, 384), whole(4, 4, 64, 384), whole(4, 4, 64, 384)
    (ret,) = call(
        group_forward_kernel, "group_forward", 1,
        [whole(4, 144, 384), a_spec, a_spec, y_spec, y_spec], [whole(4, 40, 512)],
        [array(4, 40, 512, dtype=FULL)], (zs, a, a1, y, y1),
    )
    ret = jnp.stack([ret[0]] + [swapped(ret[m], "seqlo", 8 * m) for m in (1, 2, 3)])
    attended, stat, rows, sel = call(
        merge_kernel, "merge_levels", 5,
        [COLUMNS, LANES, COLUMNS]
        + [returned_spec(part, 40) for part in range(2)]
        + [returned_spec(part, 40, 3) for part in range(2)],
        [COLUMNS, LANES, STAT_ROWS, pl.BlockSpec((2, 2, 128), lambda s, *_: (s, 0, 0))],
        [
            array(*WIDE), array(5, ROWS, 128, dtype=FULL), array(5, 8, ROWS, dtype=FULL),
            array(12, 2, 128, dtype=FULL),
        ],
        (offsets, zs_index, near, near_stat, grad_out, ret, ret, ret, ret), prefetch=2,
    )

    sel = sel.reshape(4, 3, 2, 128)
    sel_for = lambda m: lax.dynamic_index_in_dim(sel, z ^ m, 0, False)
    sel = jnp.stack([sel_for(0)] + [swapped(sel_for(m), "seqlo", 8 * m) for m in (1, 2, 3)])
    sel = two_steps(sel, "seqlo", X1, X3)
    s1 = sel[..., :32].transpose(2, 3, 0, 1, 4).reshape(3, 2, 512)
    s2 = sel[..., 32:36].transpose(2, 3, 0, 1, 4).reshape(3, 2, 64)
    s2 = jnp.stack(around(s2, "seqhi", (1, 2, 3)), 2).reshape(3, 2, 256)
    s11, s21 = core(s1), core(s2)
    sx = swapped(rows, "seqlo", X1)
    s0 = [rows, core(rows), sx, core(sx)]

    (dq_near,) = call(
        near_query_kernel, "near_query_gradient", 5, [COLUMNS] * 2 + [LANES] + [COLUMNS] * 8,
        [COLUMNS], [array(*WIDE, dtype=FULL)], (query, grad_out, stat, *keys0, *values0),
    )
    (back,) = call(
        group_backward_kernel, "group_backward", 1,
        [a_spec] * 2 + [b_spec] * 2 + [y_spec] * 2 + [whole(3, 2, 512)] * 2 + [whole(3, 2, 256)] * 2,
        [whole(4, 112, 384)], [array(4, 112, 384)],
        (a, a1, b, b1, y, y1, s1, s11, s2, s21),
    )
    back = jnp.stack([back[0]] + [swapped(back[m], "seqlo", 8 * m) for m in (1, 2, 3)])
    queries0 = [query, core(query), qx, core(qx)]
    grads0 = [grad_out, core(grad_out), gx, core(gx)]
    grad_query, grad_key, grad_value = call(
        final_kernel, "key_gradient", 5,
        [COLUMNS] * 11 + [STAT_ROWS] * 4 + [returned_spec(part, 112) for part in range(2)],
        [COLUMNS] * 3, [array(*WIDE)] * 3,
        (offsets, zs_index, key, value, dq_near, *queries0, *grads0, *s0, back, back), prefetch=2,
    )
    return attended, grad_query, grad_key, grad_value


def solution(mesh):
    spec = P(("seqhi", "seqlo"), None)
    return jax.shard_map(
        body,
        mesh=mesh,
        in_specs=(spec, spec, spec, spec, P()),
        out_specs=(spec, spec, spec, spec),
        check_vma=False,
    )
```

```python
import functools

import jax
import jax.numpy as jnp
from jax import lax
from jax.experimental import pallas as pl
from jax.experimental.pallas import tpu as pltpu
from jax.sharding import PartitionSpec as P

H = 10
HD = 128
ROWS = 256
SCALING = HD ** -0.5
LOG2E = 1.4426950408889634
FACTOR = SCALING * LOG2E
NEG = -1e30
WIDE = (ROWS, H * HD)
HALF = jnp.bfloat16
FULL = jnp.float32


def swapped(x, axis, mask):
    return lax.ppermute(x, axis, [(i, i ^ mask) for i in range(lax.axis_size(axis))])


def after(x, *others):
    return lax.optimization_barrier((x,) + others)[0]


def dot_nt(a, b):
    return lax.dot_general(a, b, (((1,), (1,)), ((), ())), preferred_element_type=FULL)


def dot_nn(a, b):
    return lax.dot_general(a, b, (((1,), (0,)), ((), ())), preferred_element_type=FULL)


def grid_ij(shape):
    return (
        lax.broadcasted_iota(jnp.int32, shape, 0),
        lax.broadcasted_iota(jnp.int32, shape, 1),
    )


def eye_column(row, n):
    i, j = grid_ij((n, n))
    return jnp.sum(jnp.where(i == j, row, 0.0), 1, keepdims=True)


def heads_of(step, parts=2):
    return [(step * parts + part, slice(part * HD, (part + 1) * HD)) for part in range(parts)]


def pick_kernel(off_ref, k_ref, v_ref, q_ref, g_ref, out_ref):
    step = pl.program_id(0)

    @pl.when(step < 5)
    def _():
        for h, cols in heads_of(step):
            i, p = grid_ij((48, ROWS))
            one = (i < 32) & (p == 8 * i + off_ref[1, h])
            two = (i >= 32) & (p == 64 * (i & 3) + off_ref[2, h])
            rows = [
                dot_nn((one | (two & ((i - 32) // 4 == t))).astype(HALF), r[:, cols])
                for t, r in enumerate((k_ref, v_ref, q_ref, g_ref))
            ]
            out_ref[0:32, cols] = rows[0][:32].astype(HALF)
            out_ref[32:64, cols] = rows[1][:32].astype(HALF)
            out_ref[64:80, cols] = sum(x[32:] for x in rows).astype(HALF)
            out_ref[80:112, cols] = rows[2][:32].astype(HALF)
            out_ref[112:144, cols] = rows[3][:32].astype(HALF)

    @pl.when(step == 5)
    def _():
        out_ref[...] = jnp.zeros(out_ref.shape, HALF)


def softmax_all(problems):
    scores = [[dot_nt(q, k) * FACTOR for k in keys] for q, keys, _ in problems]
    peaks = [
        functools.reduce(jnp.maximum, [jnp.max(s, 1, keepdims=True) for s in part])
        for part in scores
    ]
    exps = [[jnp.exp2(s - peak) for s in part] for part, peak in zip(scores, peaks)]
    totals = [sum(jnp.sum(e, 1, keepdims=True) for e in part) for part in exps]
    outs = [
        sum(dot_nn(e.astype(HALF), v) for e, v in zip(part, values))
        for part, (_, _, values) in zip(exps, problems)
    ]
    return peaks, totals, outs


def lanes_of(columns):
    _, j = grid_ij((columns[0].shape[0], 128))
    block = jnp.zeros((columns[0].shape[0], 128), FULL)
    for lane, column in enumerate(columns):
        block = jnp.where(j == lane, column, block)
    return block


def near_kernel(q_ref, *refs):
    k_refs, v_refs, (out_ref, stat_ref) = refs[:4], refs[4:8], refs[8:]
    parts = heads_of(0)
    peaks, totals, outs = softmax_all(
        [(q_ref[:, c], [k[:, c] for k in k_refs], [v[:, c] for v in v_refs]) for _, c in parts]
    )
    for (_, c), out, total in zip(parts, outs, totals):
        out_ref[:, c] = out * (1.0 / total)
    stat_ref[0] = lanes_of([peak + jnp.log2(total) for peak, total in zip(peaks, totals)])


def joined(refs, rows, c):
    return jnp.concatenate([r[:, :, rows, c].reshape(256, HD) for r in refs], 0)


def group_rows(a_ref, b_ref, y_ref, c):
    one = {
        "k": a_ref[0, :, 0:32, c], "v": a_ref[0, :, 32:64, c],
        "q": b_ref[0, :, 0:32, c], "g": b_ref[0, :, 32:64, c],
    }
    one = {name: x.reshape(128, HD) for name, x in one.items()}
    two = {name: y_ref[0, t, 0:16, c] for t, name in enumerate("kvqg")}
    return one, two


def group_forward_kernel(zs_ref, *refs):
    a0, a1, (y0_ref, y1_ref, ret_ref) = refs[0:2], refs[2:4], refs[4:]
    problems = []
    parts = heads_of(0, 3)
    for _, c in parts:
        q1 = zs_ref[:, 80:112, c].reshape(128, HD)
        problems.append((
            q1,
            [joined(r, slice(0, 32), c) for r in (a0, a1)],
            [joined(r, slice(32, 64), c) for r in (a0, a1)],
        ))
        problems.append((
            y0_ref[0, 2, 0:16, c],
            [r[:, 0, :, c].reshape(256, HD) for r in (y0_ref, y1_ref)],
            [r[:, 1, :, c].reshape(256, HD) for r in (y0_ref, y1_ref)],
        ))
    peaks, totals, outs = softmax_all(problems)
    outs = [out * (1.0 / total) for out, total in zip(outs, totals)]
    lses = [peak + jnp.log2(total) for peak, total in zip(peaks, totals)]
    one, two = lanes_of(lses[0::2]), lanes_of(lses[1::2])
    for m in range(4):
        for (_, c), out1, out2 in zip(parts, outs[0::2], outs[1::2]):
            ret_ref[m, 0:32, c] = out1[32 * m : 32 * m + 32]
            ret_ref[m, 32:36, c] = out2[4 * m : 4 * m + 4]
        ret_ref[m, 0:32, 384:512] = one[32 * m : 32 * m + 32]
        ret_ref[m, 32:36, 384:512] = two[4 * m : 4 * m + 4]
        ret_ref[m, 36:40, :] = jnp.zeros((4, 512), FULL)


def merge_kernel(off_ref, me_ref, near_ref, near_stat_ref, g_ref, ret_ref, att_ref, stat_ref, row_ref, sel_ref):
    lses, dots = [], []
    for h, c in heads_of(0, H):
        part, lane = h % 2, slice(h % 3 * HD, (h % 3 + 1) * HD)
        mine = (h // 3) ^ me_ref[0]
        p, i = grid_ij((ROWS, 40))
        hit1 = (p == 8 * i + off_ref[1, h]) & (i < 32)
        hit2 = (p == 64 * (i - 32) + off_ref[2, h]) & (i >= 32) & (i < 36)
        p, _ = grid_ij((ROWS, 1))
        chosen1 = (p & 7) == off_ref[1, h]
        chosen2 = (p & 63) == off_ref[2, h]
        lse12 = ret_ref[mine, :, 384 + h % 3 : 385 + h % 3]
        thirds = []
        for _ in range(3):
            thirds.append(lse12.astype(HALF).astype(FULL))
            lse12 = lse12 - thirds[-1]
        out12 = ret_ref[mine, :, lane]
        high = out12.astype(HALF)
        low = (out12 - high.astype(FULL)).astype(HALF)
        pieces = jnp.concatenate([high, low, lanes_of(thirds).astype(HALF)], 1)
        up1 = dot_nn(hit1.astype(HALF), pieces)
        up2 = dot_nn(hit2.astype(HALF), pieces)
        lse0 = near_stat_ref[h // 2, :, part : part + 1]
        lse1 = jnp.where(chosen1, jnp.sum(up1[:, 2 * HD :], 1, keepdims=True), NEG)
        lse2 = jnp.where(chosen2, jnp.sum(up2[:, 2 * HD :], 1, keepdims=True), NEG)
        peak = jnp.maximum(jnp.maximum(lse0, lse1), lse2)
        w0, w1, w2 = [jnp.exp2(x - peak) for x in (lse0, lse1, lse2)]
        total = w0 + w1 + w2
        out = near_ref[:, c] * w0
        out = out + (up1[:, :HD] + up1[:, HD : 2 * HD]) * w1
        out = out + (up2[:, :HD] + up2[:, HD : 2 * HD]) * w2
        out = out * (1.0 / total)
        att_ref[:, c] = out.astype(HALF)
        lses.append(peak + jnp.log2(total))
        dots.append(jnp.sum(out * g_ref[:, c].astype(FULL), 1, keepdims=True))
    for s in range(5):
        block = lanes_of(lses[2 * s : 2 * s + 2] + dots[2 * s : 2 * s + 2])
        stat_ref[s] = block
        row_ref[s] = block.T[0:8]
    for h in range(H):
        p, j = grid_ij((ROWS, 128))
        target = jnp.where(j < 32, 8 * j + off_ref[1, h], 64 * (j - 32) + off_ref[2, h])
        hit = (p == target) & (j < 36)
        sel_ref[h] = jnp.concatenate(
            [jnp.sum(jnp.where(hit, x[h], 0.0), 0, keepdims=True) for x in (lses, dots)], 0
        )
    sel_ref[H:] = jnp.zeros((12 - H, 2, 128), FULL)


def gradients(problems):
    probs = [jnp.exp2(dot_nt(a, b) * FACTOR - lse) for a, b, _, _, lse, _ in problems]
    dprobs = [dot_nt(c, d) for _, _, c, d, _, _ in problems]
    return [
        (prob.astype(HALF), (prob * (dprob - row_dot)).astype(HALF))
        for prob, dprob, (_, _, _, _, _, row_dot) in zip(probs, dprobs, problems)
    ]


def near_query_kernel(q_ref, g_ref, stat_ref, *refs):
    k_refs, v_refs, (dq_ref,) = refs[:4], refs[4:8], refs[8:]
    problems = []
    for part, (_, c) in enumerate(heads_of(0)):
        lse = stat_ref[0, :, part : part + 1]
        row_dot = stat_ref[0, :, part + 2 : part + 3]
        for k, v in zip(k_refs, v_refs):
            problems.append((q_ref[:, c], k[:, c], g_ref[:, c], v[:, c], lse, row_dot))
    done = gradients(problems)
    for part, (_, c) in enumerate(heads_of(0)):
        dq_ref[:, c] = sum(dot_nn(ds, k[:, c]) for (_, ds), k in zip(done[4 * part :], k_refs))


def gathered_stats(me_ref, s_ref, c):
    _, lane = grid_ij((8, 128))
    one = []
    two = [jnp.zeros((8, 128), FULL)] * 2
    for y in range(4):
        for x, x_mask in enumerate(MASKS4):
            block = jnp.zeros((8, 128), FULL)
            for z in range(4):
                source = (me_ref[1] ^ y) * 32 + (me_ref[2] ^ (8 * z + 2 * x_mask + c))
                rows = s_ref[source]
                if y == 0:
                    moved = pltpu.roll(rows, 32 * z, 1) if z else rows
                    block = jnp.where(lane // 32 == z, moved, block)
                start = 64 * (y % 2) + 16 * x + 4 * z
                moved = pltpu.roll(rows, (start - 32) % 128, 1) if start != 32 else rows
                two[y // 2] = jnp.where((lane >= start) & (lane < start + 4), moved, two[y // 2])
            if y == 0:
                one.append(block)
    return jnp.concatenate(one, 1), jnp.concatenate(two, 1)


def group_backward_kernel(me_ref, *refs):
    a0, a1, b0, b1 = refs[0:2], refs[2:4], refs[4:6], refs[6:8]
    y0_ref, y1_ref, s_ref, out_ref = refs[8:]
    problems, others = [], []
    parts = heads_of(0, 3)
    s10, s20 = gathered_stats(me_ref, s_ref, 0)
    s11, s21 = gathered_stats(me_ref, s_ref, 1)
    for j, c in parts:
        one, two = group_rows(a0[0], b0[0], y0_ref, c)
        sides = []
        for a, b, s in ((a0, b0, s10), (a1, b1, s11)):
            sides.append((
                joined(a, slice(0, 32), c), joined(a, slice(32, 64), c),
                joined(b, slice(0, 32), c), joined(b, slice(32, 64), c),
                s[2 * j : 2 * j + 1], s[2 * j + 1 : 2 * j + 2],
            ))
        for y, s in ((y0_ref, s20), (y1_ref, s21)):
            sides.append(
                tuple(y[:, t, :, c].reshape(256, HD) for t in range(4))
                + (s[2 * j : 2 * j + 1], s[2 * j + 1 : 2 * j + 2]))
        own = (one, one, two, two)
        for rows, n, (k, v, q, g, lse, row_dot) in zip(own, (128, 128, 16, 16), sides):
            first = sides[0] if n == 128 else sides[2]
            lse_own = eye_column(first[4][:, :n], n)
            dot_own = eye_column(first[5][:, :n], n)
            problems.append((rows["q"], k, rows["g"], v, lse_own, dot_own))
            others.append(k)
            problems.append((rows["k"], q, rows["v"], g, lse, row_dot))
            others.append((q, g))
    done = gradients(problems)
    for j, c in parts:
        mine, rest = done[8 * j : 8 * j + 8], others[8 * j : 8 * j + 8]
        dq = [dot_nn(mine[n][1], rest[n]) * SCALING for n in (0, 2, 4, 6)]
        dk = [dot_nn(mine[n][1], rest[n][0]) * SCALING for n in (1, 3, 5, 7)]
        dv = [dot_nn(mine[n][0], rest[n][1]) for n in (1, 3, 5, 7)]
        one = [(x[0] + x[1]).astype(HALF) for x in (dq, dk, dv)]
        two = [x[2] + x[3] for x in (dq, dk, dv)]
        for m in range(4):
            for t in range(3):
                out_ref[m, 32 * t : 32 * t + 32, c] = one[t][32 * m : 32 * m + 32]
            small = [x[4 * m : 4 * m + 4] for x in two] + [jnp.zeros((4, HD), FULL)]
            out_ref[m, 96:112, c] = jnp.concatenate(small, 0).astype(HALF)


def near_key_kernel(k_ref, v_ref, *refs):
    q_refs, g_refs, s_refs, (dk_ref, dv_ref) = refs[:4], refs[4:8], refs[8:12], refs[12:]
    problems = []
    for part, (_, c) in enumerate(heads_of(0)):
        for q, g, s in zip(q_refs, g_refs, s_refs):
            lse, row_dot = s[0, part : part + 1, :], s[0, part + 2 : part + 3, :]
            problems.append((k_ref[:, c], q[:, c], v_ref[:, c], g[:, c], lse, row_dot))
    done = gradients(problems)
    for part, (_, c) in enumerate(heads_of(0)):
        mine = done[4 * part : 4 * part + 4]
        dk_ref[:, c] = sum(dot_nn(ds, q[:, c]) for (_, ds), q in zip(mine, q_refs))
        dv_ref[:, c] = sum(dot_nn(prob, g[:, c]) for (prob, _), g in zip(mine, g_refs))


def add_kernel(off_ref, me_ref, dq_near_ref, dk_near_ref, dv_near_ref, back_ref, dq_ref, dk_ref, dv_ref):
    p, r = grid_ij((ROWS, 112))
    tensor = jnp.where(r < 96, r // 32, (r - 96) // 4)
    for h, c in heads_of(0, H):
        target = jnp.where(r < 96, 8 * (r & 31) + off_ref[1, h], 64 * (r & 3) + off_ref[2, h])
        hit = p == target
        rows = back_ref[(h // 3) ^ me_ref[0], :, h % 3 * HD : (h % 3 + 1) * HD]
        lifted = [dot_nn((hit & (tensor == t)).astype(HALF), rows) for t in range(3)]
        dq_ref[:, c] = (dq_near_ref[:, c] * SCALING + lifted[0]).astype(HALF)
        dk_ref[:, c] = (dk_near_ref[:, c] * SCALING + lifted[1]).astype(HALF)
        dv_ref[:, c] = (dv_near_ref[:, c] + lifted[2]).astype(HALF)


COLUMNS = pl.BlockSpec((ROWS, 2 * HD), lambda s, *_: (0, s))
LANES = pl.BlockSpec((1, ROWS, 128), lambda s, *_: (s, 0, 0))
STAT_ROWS = pl.BlockSpec((1, 8, ROWS), lambda s, *_: (s, 0, 0))


def whole(*shape):
    return pl.BlockSpec(shape, lambda *_: (0,) * len(shape))


def array(*shape, dtype=HALF):
    return jax.ShapeDtypeStruct(shape, dtype)


def call(kernel, name, steps, in_specs, out_specs, out_shape, operands, prefetch=0, room=60, time=0.001):
    return pl.pallas_call(
        kernel,
        grid_spec=pltpu.PrefetchScalarGridSpec(
            num_scalar_prefetch=prefetch, grid=(steps,), in_specs=in_specs, out_specs=out_specs
        ),
        out_shape=out_shape,
        compiler_params=pltpu.CompilerParams(vmem_limit_bytes=room * 1024 * 1024),
        cost_estimate=pl.CostEstimate(flops=int(time * 1_150_000_000), bytes_accessed=100_000, transcendentals=0),
        name=name,
    )(*operands)


CORE, X1, X3 = 1, 2, 6
MASKS4 = (0, 1, 3, 2)
ZS = (8, 16, 24)


def two_steps(x, axis, first, second):
    x = jnp.stack([x, swapped(x, axis, first)])
    return jnp.concatenate([x, swapped(x, axis, second)], 0)


def around(x, axis, masks):
    return [x] + [swapped(x, axis, m) for m in masks]


def core(x):
    return swapped(x, "seqlo", CORE)


def body(query, key, value, grad_out, offsets):
    z = lax.axis_index("seqlo") // 8
    me = jnp.stack([z, lax.axis_index("seqhi"), lax.axis_index("seqlo")]).astype(jnp.int32)
    kx = swapped(key, "seqlo", X1)
    picked = call(
        pick_kernel, "pick_rows", 6,
        [pl.BlockSpec((ROWS, 2 * HD), lambda s, *_: (0, jnp.minimum(s, 4)))] * 4,
        [pl.BlockSpec((144, 2 * HD), lambda s, *_: (0, s))],
        [array(144, 12 * HD)],
        (offsets, key, value, query, grad_out), prefetch=1,
    )[0]

    def for_z(x, m, width):
        return lax.dynamic_slice_in_dim(x, (z ^ m) * width, width, x.ndim - 1)

    zs = jnp.stack(
        [for_z(picked, 0, 384)]
        + [swapped(for_z(picked, m, 384), "seqlo", 8 * m) for m in (1, 2, 3)]
    )
    a, y, _ = lax.optimization_barrier((zs[:, :64], zs[:, 64:80], kx))
    y = jnp.stack([y, swapped(y, "seqlo", X1)])
    a = jnp.stack([a, swapped(a, "seqlo", X1)])
    vx = swapped(after(value, a, y), "seqlo", X1)
    y = jnp.concatenate([y, swapped(y, "seqlo", X3)], 0)
    a3 = swapped(a, "seqlo", X3)
    y = y.reshape(4, 4, 4, 4, 384).transpose(2, 0, 1, 3, 4).reshape(4, 64, 384)
    vx, a, a3, y = lax.optimization_barrier((vx, a, a3, y))
    b = after(zs[:, 80:], vx)
    b = jnp.stack([b, swapped(b, "seqlo", X1)])
    qx = swapped(after(query, b), "seqlo", X1)
    gx = swapped(after(grad_out, b), "seqlo", X1)
    y = around(y, "seqhi", (1, 2, 3))
    y = jnp.stack(lax.optimization_barrier((*y, b))[:4])
    keys0 = [key, core(key), kx, core(kx)]
    values0 = [value, core(value), vx, core(vx)]
    a, y = [a, a3, core(a), core(a3)], [y, core(y)]
    part_spec, y_spec = whole(2, 4, 64, 384), whole(4, 4, 64, 384)
    (ret,) = call(
        group_forward_kernel, "group_forward", 1,
        [whole(4, 144, 384)] + [part_spec] * 4 + [y_spec] * 2, [whole(4, 40, 512)],
        [array(4, 40, 512, dtype=FULL)], (zs, *a, *y),
    )
    near, near_stat = call(
        near_kernel, "near_forward", 5, [COLUMNS] * 9, [COLUMNS, LANES],
        [array(*WIDE, dtype=FULL), array(5, ROWS, 128, dtype=FULL)],
        (after(query, ret), *keys0, *values0),
    )
    b3 = swapped(after(b, near_stat), "seqlo", X3)
    ret = [ret[0]] + [swapped(ret[m], "seqlo", 8 * m) for m in (1, 2, 3)]
    ret = jnp.stack(lax.optimization_barrier((*ret, near_stat, qx))[:4])
    attended, stat, rows, sel = call(
        merge_kernel, "merge_levels", 1,
        [whole(*WIDE), whole(5, ROWS, 128), whole(*WIDE), whole(4, 40, 512)],
        [whole(*WIDE), whole(5, ROWS, 128), whole(5, 8, ROWS), whole(12, 2, 128)],
        [
            array(*WIDE), array(5, ROWS, 128, dtype=FULL), array(5, 8, ROWS, dtype=FULL),
            array(12, 2, 128, dtype=FULL),
        ],
        (offsets, me, near, near_stat, grad_out, ret), prefetch=2,
    )

    sel = sel.reshape(1, 4, 1, 6, 128)
    sel = jnp.pad(sel, ((0, 0),) * 3 + ((0, 2), (0, 0)))
    sel = jnp.broadcast_to(sel, (4, 4, 8, 8, 128)).reshape(128, 8, 128)
    sel = lax.all_to_all(sel, ("seqhi", "seqlo"), 0, 0, tiled=True)
    b, b3 = lax.optimization_barrier((b, b3, rows))[:2]
    b = [b, b3, core(b), core(b3)]
    sx = swapped(rows, "seqlo", X1)
    queries0 = [query, core(query), qx, core(qx)]
    grads0 = [grad_out, core(grad_out), gx, core(gx)]
    (dq_near,) = call(
        near_query_kernel, "near_query_gradient", 5, [COLUMNS] * 2 + [LANES] + [COLUMNS] * 8,
        [COLUMNS], [array(*WIDE, dtype=FULL)],
        (query, grad_out, after(stat, gx), *keys0, *values0), time=8,
    )
    sel = after(sel, dq_near)
    (back,) = call(
        group_backward_kernel, "group_backward", 1,
        [part_spec] * 8 + [y_spec] * 2 + [whole(128, 8, 128)],
        [whole(4, 112, 384)], [array(4, 112, 384)],
        (me, *a, *b, *y, sel), prefetch=1,
    )
    sx = after(sx, back)
    s0 = [rows, core(rows), sx, core(sx)]
    dk_near, dv_near = call(
        near_key_kernel, "near_key_gradient", 5, [COLUMNS] * 10 + [STAT_ROWS] * 4, [COLUMNS] * 2,
        [array(*WIDE, dtype=FULL)] * 2, (key, value, *queries0, *grads0, *s0),
    )
    back = [back[0]] + [swapped(back[m], "seqlo", 8 * m) for m in (1, 2, 3)]
    back = jnp.stack(lax.optimization_barrier((*back, dk_near))[:4])
    grad_query, grad_key, grad_value = call(
        add_kernel, "add_levels", 1,
        [whole(*WIDE)] * 3 + [whole(4, 112, 384)], [whole(*WIDE)] * 3, [array(*WIDE)] * 3,
        (offsets, me, dq_near, dk_near, dv_near, back), prefetch=2,
    )
    return attended, grad_query, grad_key, grad_value


def solution(mesh):
    spec = P(("seqhi", "seqlo"), None)
    return jax.shard_map(
        body,
        mesh=mesh,
        in_specs=(spec, spec, spec, spec, P()),
        out_specs=(spec, spec, spec, spec),
        check_vma=False,
    )
```

```python
import functools

import jax
import jax.numpy as jnp
from jax import lax
from jax.experimental import pallas as pl
from jax.experimental.pallas import tpu as pltpu
from jax.sharding import PartitionSpec as P

H = 10
HD = 128
ROWS = 256
SCALING = HD ** -0.5
LOG2E = 1.4426950408889634
FACTOR = SCALING * LOG2E
NEG = -1e30
WIDE = (ROWS, H * HD)
HALF = jnp.bfloat16
FULL = jnp.float32


def swapped(x, axis, mask):
    return lax.ppermute(x, axis, [(i, i ^ mask) for i in range(lax.axis_size(axis))])


def together(*arrays):
    return lax.optimization_barrier(arrays)


def dot_nt(a, b):
    return lax.dot_general(a, b, (((1,), (1,)), ((), ())), preferred_element_type=FULL)


def dot_nn(a, b):
    return lax.dot_general(a, b, (((1,), (0,)), ((), ())), preferred_element_type=FULL)


def grid_ij(shape):
    return (
        lax.broadcasted_iota(jnp.int32, shape, 0),
        lax.broadcasted_iota(jnp.int32, shape, 1),
    )


def eye_column(row, n):
    i, j = grid_ij((n, n))
    return jnp.sum(jnp.where(i == j, row, 0.0), 1, keepdims=True)


def heads_of(step, parts=2):
    return [(step * parts + part, slice(part * HD, (part + 1) * HD)) for part in range(parts)]


def pick_kernel(off_ref, me_ref, k_ref, v_ref, q_ref, g_ref, *out_refs):
    i, p = grid_ij((48, ROWS))
    for m, out_ref in enumerate(out_refs):
        for j, cols in heads_of(0, 3):
            head = 3 * (me_ref[0] ^ m) + j
            h = jnp.minimum(head, H - 1)
            lanes = pl.ds(pl.multiple_of(h * HD, HD), HD)
            one = (i < 32) & (p == 8 * i + off_ref[1, h]) & (head < H)
            two = (i >= 32) & (p == 64 * (i & 3) + off_ref[2, h]) & (head < H)
            rows = [
                dot_nn((one | (two & ((i - 32) // 4 == t))).astype(HALF), r[:, lanes])
                for t, r in enumerate((k_ref, v_ref, q_ref, g_ref))
            ]
            out_ref[0:32, cols] = rows[0][:32].astype(HALF)
            out_ref[32:64, cols] = rows[1][:32].astype(HALF)
            out_ref[64:80, cols] = sum(x[32:] for x in rows).astype(HALF)
            out_ref[80:112, cols] = rows[2][:32].astype(HALF)
            out_ref[112:144, cols] = rows[3][:32].astype(HALF)


def softmax_all(problems):
    scores = [[dot_nt(q, k) * FACTOR for k in keys] for q, keys, _ in problems]
    peaks = [
        functools.reduce(jnp.maximum, [jnp.max(s, 1, keepdims=True) for s in part])
        for part in scores
    ]
    exps = [[jnp.exp2(s - peak) for s in part] for part, peak in zip(scores, peaks)]
    totals = [sum(jnp.sum(e, 1, keepdims=True) for e in part) for part in exps]
    outs = [
        sum(dot_nn(e.astype(HALF), v) for e, v in zip(part, values))
        for part, (_, _, values) in zip(exps, problems)
    ]
    return peaks, totals, outs


def lanes_of(columns):
    _, j = grid_ij((columns[0].shape[0], 128))
    block = jnp.zeros((columns[0].shape[0], 128), FULL)
    for lane, column in enumerate(columns):
        block = jnp.where(j == lane, column, block)
    return block


def near_kernel(q_ref, *refs):
    k_refs, v_refs, (out_ref, stat_ref) = refs[:4], refs[4:8], refs[8:]
    parts = heads_of(0, 5)
    peaks, totals, outs = softmax_all(
        [(q_ref[:, c], [k[:, c] for k in k_refs], [v[:, c] for v in v_refs]) for _, c in parts]
    )
    for (_, c), out, total in zip(parts, outs, totals):
        out_ref[:, c] = out * (1.0 / total)
    block = lanes_of([peak + jnp.log2(total) for peak, total in zip(peaks, totals)])
    stat_ref[0] = block.T[0:8]


def joined(refs, rows, c):
    return jnp.concatenate([r[:, :, rows, c].reshape(256, HD) for r in refs], 0)


def group_rows(a_ref, b_ref, y_ref, c):
    one = {
        "k": a_ref[0, :, 0:32, c], "v": a_ref[0, :, 32:64, c],
        "q": b_ref[0, :, 0:32, c], "g": b_ref[0, :, 32:64, c],
    }
    one = {name: x.reshape(128, HD) for name, x in one.items()}
    two = {name: y_ref[0, t, 0:16, c] for t, name in enumerate("kvqg")}
    return one, two


def group_forward_kernel(zs_ref, *refs):
    a0, a1, (y0_ref, y1_ref), ret_refs = refs[0:2], refs[2:4], refs[4:6], refs[6:]
    problems = []
    parts = heads_of(0, 3)
    for _, c in parts:
        q1 = zs_ref[:, 80:112, c].reshape(128, HD)
        problems.append((
            q1,
            [joined(r, slice(0, 32), c) for r in (a0, a1)],
            [joined(r, slice(32, 64), c) for r in (a0, a1)],
        ))
        problems.append((
            y0_ref[0, 2, 0:16, c],
            [r[:, 0, :, c].reshape(256, HD) for r in (y0_ref, y1_ref)],
            [r[:, 1, :, c].reshape(256, HD) for r in (y0_ref, y1_ref)],
        ))
    peaks, totals, outs = softmax_all(problems)
    outs = [out * (1.0 / total) for out, total in zip(outs, totals)]
    lses = [peak + jnp.log2(total) for peak, total in zip(peaks, totals)]
    one, two = lanes_of(lses[0::2]), lanes_of(lses[1::2])
    for m, ret_ref in enumerate(ret_refs):
        for (_, c), out1, out2 in zip(parts, outs[0::2], outs[1::2]):
            ret_ref[0:32, c] = out1[32 * m : 32 * m + 32]
            ret_ref[32:36, c] = out2[4 * m : 4 * m + 4]
        ret_ref[0:32, 384:512] = one[32 * m : 32 * m + 32]
        ret_ref[32:36, 384:512] = two[4 * m : 4 * m + 4]
        ret_ref[36:40, :] = jnp.zeros((4, 512), FULL)


def thirds_of(x):
    pieces = []
    for _ in range(3):
        pieces.append(x.astype(HALF))
        x = x - pieces[-1].astype(FULL)
    return pieces


def row_times(row, onehot):
    i, _ = grid_ij((8, row.shape[1]))
    rows = jnp.zeros((8, row.shape[1]), FULL)
    for n, piece in enumerate(thirds_of(row)):
        rows = jnp.where(i == n, piece.astype(FULL), rows)
    return jnp.sum(dot_nn(rows.astype(HALF), onehot), 0, keepdims=True)


def transposed(rows):
    rows = list(rows)
    width = rows[0].shape[1]
    return jnp.concatenate(rows + [jnp.zeros((128 - len(rows), width), FULL)], 0).T


def merge_kernel(off_ref, me_ref, near_ref, near_stat_ref, g_ref, ret_ref, att_ref, stat_ref, row_ref, sel_ref):
    lses, scales, picked, far_scales, hits = [], [], [], [], []
    for h in range(H):
        mine = (h // 3) ^ me_ref[0]
        i, p = grid_ij((40, ROWS))
        one = (i < 32) & (p == 8 * i + off_ref[1, h])
        two = (i >= 32) & (i < 36) & (p == 64 * (i - 32) + off_ref[2, h])
        far = ret_ref[mine, :, 384:512].T[h % 3 : h % 3 + 1]
        both = row_times(far, jnp.concatenate([one, two], 1).astype(HALF))
        _, p = grid_ij((1, ROWS))
        lse0 = near_stat_ref[h // 5, h % 5 : h % 5 + 1, :]
        lse1 = jnp.where((p & 7) == off_ref[1, h], both[:, :ROWS], NEG)
        lse2 = jnp.where((p & 63) == off_ref[2, h], both[:, ROWS:], NEG)
        peak = jnp.maximum(jnp.maximum(lse0, lse1), lse2)
        total = jnp.exp2(lse0 - peak) + jnp.exp2(lse1 - peak) + jnp.exp2(lse2 - peak)
        lses.append(peak + jnp.log2(total))
        scales.append(jnp.exp2(lse0 - lses[-1]))
        p, j = grid_ij((ROWS, 128))
        target = jnp.where(j < 32, 8 * j + off_ref[1, h], 64 * (j - 32) + off_ref[2, h])
        hits.append(((p == target) & (j < 36)).astype(HALF))
        picked.append(row_times(lses[-1], hits[-1]))
        _, j = grid_ij((1, 40))
        far_scale = jnp.where(j < 36, jnp.exp2(jnp.minimum(far - picked[-1][:, :40], 1.0)), 0.0)
        far_scales.append(jnp.concatenate([far_scale, jnp.zeros((1, 88), FULL)], 1))
    scales = transposed(scales)
    far_scales = transposed(far_scales)
    dots = []
    for h, c in heads_of(0, H):
        mine, lane = (h // 3) ^ me_ref[0], slice(h % 3 * HD, (h % 3 + 1) * HD)
        far = ret_ref[mine, :, lane] * far_scales[:40, h : h + 1]
        high = far.astype(HALF)
        low = (far - high.astype(FULL)).astype(HALF)
        lifted = dot_nn(hits[h][:, :40], jnp.concatenate([high, low], 1))
        out = near_ref[:, c] * scales[:, h : h + 1] + lifted[:, :HD] + lifted[:, HD:]
        att_ref[:, c] = out.astype(HALF)
        dots.append(jnp.sum(out * g_ref[:, c].astype(FULL), 1, keepdims=True))
    dots = lanes_of(dots).T
    dots = [dots[h : h + 1] for h in range(H)]
    for s in range(2):
        stat_ref[s] = transposed(lses[5 * s : 5 * s + 5] + dots[5 * s : 5 * s + 5])
    for s in range(5):
        rows = lses[2 * s : 2 * s + 2] + dots[2 * s : 2 * s + 2]
        row_ref[s] = jnp.concatenate(rows + [jnp.zeros((4, ROWS), FULL)], 0)
    rows = []
    for h in range(H):
        rows += [picked[h], row_times(dots[h], hits[h])]
    rows += [jnp.zeros((1, 128), FULL)] * (24 - 2 * H)
    for z in range(4):
        block = jnp.concatenate(rows[6 * z : 6 * z + 6] + [jnp.zeros((2, 128), FULL)], 0)
        for i in range(32):
            sel_ref[i // 8 * 32 + 8 * z + i % 8] = block


def gradients(problems):
    probs = [jnp.exp2(dot_nt(a, b) * FACTOR - lse) for a, b, _, _, lse, _ in problems]
    dprobs = [dot_nt(c, d) for _, _, c, d, _, _ in problems]
    return [
        (prob.astype(HALF), (prob * (dprob - row_dot)).astype(HALF))
        for prob, dprob, (_, _, _, _, _, row_dot) in zip(probs, dprobs, problems)
    ]


def near_query_kernel(q_ref, g_ref, stat_ref, *refs):
    k_refs, v_refs, (dq_ref,) = refs[:4], refs[4:8], refs[8:]
    problems = []
    for part, (_, c) in enumerate(heads_of(0, 5)):
        lse = stat_ref[0, :, part : part + 1]
        row_dot = stat_ref[0, :, part + 5 : part + 6]
        for k, v in zip(k_refs, v_refs):
            problems.append((q_ref[:, c], k[:, c], g_ref[:, c], v[:, c], lse, row_dot))
    done = gradients(problems)
    for part, (_, c) in enumerate(heads_of(0, 5)):
        dq_ref[:, c] = sum(dot_nn(ds, k[:, c]) for (_, ds), k in zip(done[4 * part :], k_refs))


def gathered_stats(me_ref, s_ref, c):
    _, lane = grid_ij((8, 128))
    one = []
    two = [jnp.zeros((8, 128), FULL)] * 2
    for y in range(4):
        for x, x_mask in enumerate(MASKS4):
            block = jnp.zeros((8, 128), FULL)
            for z in range(4):
                source = (me_ref[1] ^ y) * 32 + (me_ref[2] ^ (8 * z + 2 * x_mask + c))
                rows = s_ref[source]
                if y == 0:
                    moved = pltpu.roll(rows, 32 * z, 1) if z else rows
                    block = jnp.where(lane // 32 == z, moved, block)
                start = 64 * (y % 2) + 16 * x + 4 * z
                moved = pltpu.roll(rows, (start - 32) % 128, 1) if start != 32 else rows
                two[y // 2] = jnp.where((lane >= start) & (lane < start + 4), moved, two[y // 2])
            if y == 0:
                one.append(block)
    return jnp.concatenate(one, 1), jnp.concatenate(two, 1)


def group_backward_kernel(me_ref, *refs):
    a0, a1, b0, b1 = refs[0:2], refs[2:4], refs[4:6], refs[6:8]
    (y0_ref, y1_ref, s_ref), out_refs = refs[8:11], refs[11:]
    problems, others = [], []
    parts = heads_of(0, 3)
    s10, s20 = gathered_stats(me_ref, s_ref, 0)
    s11, s21 = gathered_stats(me_ref, s_ref, 1)
    for j, c in parts:
        one, two = group_rows(a0[0], b0[0], y0_ref, c)
        sides = []
        for a, b, s in ((a0, b0, s10), (a1, b1, s11)):
            sides.append((
                joined(a, slice(0, 32), c), joined(a, slice(32, 64), c),
                joined(b, slice(0, 32), c), joined(b, slice(32, 64), c),
                s[2 * j : 2 * j + 1], s[2 * j + 1 : 2 * j + 2],
            ))
        for y, s in ((y0_ref, s20), (y1_ref, s21)):
            sides.append(
                tuple(y[:, t, :, c].reshape(256, HD) for t in range(4))
                + (s[2 * j : 2 * j + 1], s[2 * j + 1 : 2 * j + 2]))
        own = (one, one, two, two)
        for rows, n, (k, v, q, g, lse, row_dot) in zip(own, (128, 128, 16, 16), sides):
            first = sides[0] if n == 128 else sides[2]
            lse_own = eye_column(first[4][:, :n], n)
            dot_own = eye_column(first[5][:, :n], n)
            problems.append((rows["q"], k, rows["g"], v, lse_own, dot_own))
            others.append(k)
            problems.append((rows["k"], q, rows["v"], g, lse, row_dot))
            others.append((q, g))
    done = gradients(problems)
    for j, c in parts:
        mine, rest = done[8 * j : 8 * j + 8], others[8 * j : 8 * j + 8]
        dq = [dot_nn(mine[n][1], rest[n]) * SCALING for n in (0, 2, 4, 6)]
        dk = [dot_nn(mine[n][1], rest[n][0]) * SCALING for n in (1, 3, 5, 7)]
        dv = [dot_nn(mine[n][0], rest[n][1]) for n in (1, 3, 5, 7)]
        one = [(x[0] + x[1]).astype(HALF) for x in (dq, dk, dv)]
        two = [x[2] + x[3] for x in (dq, dk, dv)]
        for m, out_ref in enumerate(out_refs):
            for t in range(3):
                out_ref[32 * t : 32 * t + 32, c] = one[t][32 * m : 32 * m + 32]
            small = [x[4 * m : 4 * m + 4] for x in two] + [jnp.zeros((4, HD), FULL)]
            out_ref[96:112, c] = jnp.concatenate(small, 0).astype(HALF)


def near_key_kernel(k_ref, v_ref, *refs):
    q_refs, g_refs, s_refs, (dk_ref, dv_ref) = refs[:4], refs[4:8], refs[8:12], refs[12:]
    problems = []
    for part, (_, c) in enumerate(heads_of(0)):
        for q, g, s in zip(q_refs, g_refs, s_refs):
            lse, row_dot = s[0, part : part + 1, :], s[0, part + 2 : part + 3, :]
            problems.append((k_ref[:, c], q[:, c], v_ref[:, c], g[:, c], lse, row_dot))
    done = gradients(problems)
    for part, (_, c) in enumerate(heads_of(0)):
        mine = done[4 * part : 4 * part + 4]
        dk_ref[:, c] = sum(dot_nn(ds, q[:, c]) for (_, ds), q in zip(mine, q_refs))
        dv_ref[:, c] = sum(dot_nn(prob, g[:, c]) for (prob, _), g in zip(mine, g_refs))


def add_kernel(off_ref, me_ref, dq_near_ref, dk_near_ref, dv_near_ref, back_ref, dq_ref, dk_ref, dv_ref):
    p, r = grid_ij((ROWS, 112))
    tensor = jnp.where(r < 96, r // 32, (r - 96) // 4)
    for h, c in heads_of(0, H):
        target = jnp.where(r < 96, 8 * (r & 31) + off_ref[1, h], 64 * (r & 3) + off_ref[2, h])
        hit = p == target
        rows = back_ref[(h // 3) ^ me_ref[0], :, h % 3 * HD : (h % 3 + 1) * HD]
        lifted = [dot_nn((hit & (tensor == t)).astype(HALF), rows) for t in range(3)]
        dq_ref[:, c] = (dq_near_ref[:, c] * SCALING + lifted[0]).astype(HALF)
        dk_ref[:, c] = (dk_near_ref[:, c] * SCALING + lifted[1]).astype(HALF)
        dv_ref[:, c] = (dv_near_ref[:, c] + lifted[2]).astype(HALF)


COLUMNS = pl.BlockSpec((ROWS, 2 * HD), lambda s, *_: (0, s))
FIVE = pl.BlockSpec((ROWS, 5 * HD), lambda s, *_: (0, s))
LANES = pl.BlockSpec((1, ROWS, 128), lambda s, *_: (s, 0, 0))
STAT_ROWS = pl.BlockSpec((1, 8, ROWS), lambda s, *_: (s, 0, 0))


def whole(*shape):
    return pl.BlockSpec(shape, lambda *_: (0,) * len(shape))


def array(*shape, dtype=HALF):
    return jax.ShapeDtypeStruct(shape, dtype)


def call(kernel, name, steps, in_specs, out_specs, out_shape, operands, prefetch=0, room=60, time=0.001):
    return pl.pallas_call(
        kernel,
        grid_spec=pltpu.PrefetchScalarGridSpec(
            num_scalar_prefetch=prefetch, grid=(steps,), in_specs=in_specs, out_specs=out_specs
        ),
        out_shape=out_shape,
        compiler_params=pltpu.CompilerParams(vmem_limit_bytes=room * 1024 * 1024),
        cost_estimate=pl.CostEstimate(flops=int(time * 1_150_000_000), bytes_accessed=100_000, transcendentals=0),
        name=name,
    )(*operands)


CORE, X1, X3 = 1, 2, 6
MASKS4 = (0, 1, 3, 2)
ZS = (8, 16, 24)


def two_steps(x, axis, first, second):
    x = jnp.stack([x, swapped(x, axis, first)])
    return jnp.concatenate([x, swapped(x, axis, second)], 0)


def around(x, axis, masks):
    return [x] + [swapped(x, axis, m) for m in masks]


def over_z(parts):
    return [parts[0]] + [swapped(parts[m], "seqlo", 8 * m) for m in (1, 2, 3)]


def core(x):
    return swapped(x, "seqlo", CORE)


def body(query, key, value, grad_out, offsets):
    z = lax.axis_index("seqlo") // 8
    me = jnp.stack([z, lax.axis_index("seqhi"), lax.axis_index("seqlo")]).astype(jnp.int32)
    kx = swapped(key, "seqlo", X1)
    zs = call(
        pick_kernel, "pick_rows", 1, [whole(*WIDE)] * 4, [whole(144, 384)] * 4,
        [array(144, 384)] * 4, (offsets, me, key, value, query, grad_out), prefetch=2,
    )
    zs = jnp.stack(over_z(zs))
    a, y, b, kx = together(zs[:, :64], zs[:, 64:80], zs[:, 80:], kx)
    y = jnp.stack([y, swapped(y, "seqlo", X1)])
    a, y, b = together(a, y, b)
    a, b = [jnp.stack([t, swapped(t, "seqlo", X1)]) for t in (a, b)]
    y = jnp.concatenate([y, swapped(y, "seqlo", X3)], 0)
    value_out, a, b = together(value, a, b)
    vx = swapped(value_out, "seqlo", X1)
    a, y = together(a, y)
    a3 = swapped(a, "seqlo", X3)
    y = y.reshape(4, 4, 4, 4, 384).transpose(2, 0, 1, 3, 4).reshape(4, 64, 384)
    y = around(y, "seqhi", (1, 2, 3))
    a3, *y = together(a3, *y)
    b3 = swapped(b, "seqlo", X3)
    both = jnp.stack([query, grad_out])
    both, vx = together(both, vx)
    both = swapped(both, "seqlo", X1)
    y = jnp.stack(y)
    a, y = [a, a3, core(a), core(a3)], [y, core(y)]
    part_spec, y_spec = whole(2, 4, 64, 384), whole(4, 4, 64, 384)
    ret = call(
        group_forward_kernel, "group_forward", 1,
        [whole(4, 144, 384)] + [part_spec] * 4 + [y_spec] * 2, [whole(40, 512)] * 4,
        [array(40, 512, dtype=FULL)] * 4, (zs, *a, *y),
    )
    ret = over_z(ret)
    near_query, ret[1] = together(query, ret[1])
    keys0 = [key, core(key), kx, core(kx)]
    values0 = [value, core(value), vx, core(vx)]
    near, near_stat = call(
        near_kernel, "near_forward", 2, [FIVE] * 9, [FIVE, STAT_ROWS],
        [array(*WIDE, dtype=FULL), array(2, 8, ROWS, dtype=FULL)],
        (near_query, *keys0, *values0),
    )
    *ret, near_stat, b3 = together(*ret, near_stat, b3)
    ret = jnp.stack(ret)
    attended, stat, rows, sel = call(
        merge_kernel, "merge_levels", 1,
        [whole(*WIDE), whole(2, 8, ROWS), whole(*WIDE), whole(4, 40, 512)],
        [whole(*WIDE), whole(2, ROWS, 128), whole(5, 8, ROWS), whole(128, 8, 128)],
        [
            array(*WIDE), array(2, ROWS, 128, dtype=FULL), array(5, 8, ROWS, dtype=FULL),
            array(128, 8, 128, dtype=FULL),
        ],
        (offsets, me, near, near_stat, grad_out, ret), prefetch=2,
    )

    sel = lax.all_to_all(sel, ("seqhi", "seqlo"), 0, 0, tiled=True)
    b = [b, b3, core(b), core(b3)]
    sx = swapped(rows, "seqlo", X1)
    stat, both = together(stat, both)
    qx, gx = both[0], both[1]
    queries0 = [query, core(query), qx, core(qx)]
    grads0 = [grad_out, core(grad_out), gx, core(gx)]
    (dq_near,) = call(
        near_query_kernel, "near_query_gradient", 2, [FIVE] * 2 + [LANES] + [FIVE] * 8,
        [FIVE], [array(*WIDE, dtype=FULL)],
        (query, grad_out, stat, *keys0, *values0), time=8,
    )
    sel, dq_near = together(sel, dq_near)
    back = call(
        group_backward_kernel, "group_backward", 1,
        [part_spec] * 8 + [y_spec] * 2 + [whole(128, 8, 128)],
        [whole(112, 384)] * 4, [array(112, 384)] * 4,
        (me, *a, *b, *y, sel), prefetch=1,
    )
    sx, *back = together(sx, *back)
    s0 = [rows, core(rows), sx, core(sx)]
    dk_near, dv_near = call(
        near_key_kernel, "near_key_gradient", 5, [COLUMNS] * 10 + [STAT_ROWS] * 4, [COLUMNS] * 2,
        [array(*WIDE, dtype=FULL)] * 2, (key, value, *queries0, *grads0, *s0),
    )
    back = over_z(back)
    *back, dk_near = together(*back, dk_near)
    back = jnp.stack(back)
    grad_query, grad_key, grad_value = call(
        add_kernel, "add_levels", 1,
        [whole(*WIDE)] * 3 + [whole(4, 112, 384)], [whole(*WIDE)] * 3, [array(*WIDE)] * 3,
        (offsets, me, dq_near, dk_near, dv_near, back), prefetch=2,
    )
    return attended, grad_query, grad_key, grad_value


def solution(mesh):
    spec = P(("seqhi", "seqlo"), None)
    return jax.shard_map(
        body,
        mesh=mesh,
        in_specs=(spec, spec, spec, spec, P()),
        out_specs=(spec, spec, spec, spec),
        check_vma=False,
    )
```

```python
import functools

import jax
import jax.numpy as jnp
from jax import lax
from jax.experimental import pallas as pl
from jax.experimental.pallas import tpu as pltpu
from jax.sharding import PartitionSpec as P

H = 10
HD = 128
ROWS = 256
SCALING = HD ** -0.5
LOG2E = 1.4426950408889634
FACTOR = SCALING * LOG2E
NEG = -1e30
WIDE = (ROWS, H * HD)
HALF = jnp.bfloat16
FULL = jnp.float32


def swapped(x, axis, mask):
    return lax.ppermute(x, axis, [(i, i ^ mask) for i in range(lax.axis_size(axis))])


def together(*arrays):
    return lax.optimization_barrier(arrays)


def dot_nt(a, b):
    return lax.dot_general(a, b, (((1,), (1,)), ((), ())), preferred_element_type=FULL)


def dot_nn(a, b):
    return lax.dot_general(a, b, (((1,), (0,)), ((), ())), preferred_element_type=FULL)


def grid_ij(shape):
    return (
        lax.broadcasted_iota(jnp.int32, shape, 0),
        lax.broadcasted_iota(jnp.int32, shape, 1),
    )


def eye_column(row, n):
    i, j = grid_ij((n, n))
    return jnp.sum(jnp.where(i == j, row, 0.0), 1, keepdims=True)


def heads_of(step, parts=2):
    return [(step * parts + part, slice(part * HD, (part + 1) * HD)) for part in range(parts)]


def pick_kernel(off_ref, k_ref, v_ref, q_ref, g_ref, out_ref):
    i, p = grid_ij((48, ROWS))
    out_ref[3, :, HD:] = jnp.zeros((144, 2 * HD), HALF)
    for h, lanes in heads_of(0, H):
        z, cols = h // 3, slice(h % 3 * HD, (h % 3 + 1) * HD)
        one = (i < 32) & (p == 8 * i + off_ref[1, h])
        two = (i >= 32) & (p == 64 * (i & 3) + off_ref[2, h])
        rows = [
            dot_nn((one | (two & ((i - 32) // 4 == t))).astype(HALF), r[:, lanes])
            for t, r in enumerate((k_ref, v_ref, q_ref, g_ref))
        ]
        out_ref[z, 0:32, cols] = rows[0][:32].astype(HALF)
        out_ref[z, 32:64, cols] = rows[1][:32].astype(HALF)
        out_ref[z, 64:80, cols] = sum(x[32:] for x in rows).astype(HALF)
        out_ref[z, 80:112, cols] = rows[2][:32].astype(HALF)
        out_ref[z, 112:144, cols] = rows[3][:32].astype(HALF)


def softmax_all(problems):
    scores = [[dot_nt(q, k) * FACTOR for k in keys] for q, keys, _ in problems]
    peaks = [
        functools.reduce(jnp.maximum, [jnp.max(s, 1, keepdims=True) for s in part])
        for part in scores
    ]
    exps = [[jnp.exp2(s - peak) for s in part] for part, peak in zip(scores, peaks)]
    totals = [sum(jnp.sum(e, 1, keepdims=True) for e in part) for part in exps]
    outs = [
        sum(dot_nn(e.astype(HALF), v) for e, v in zip(part, values))
        for part, (_, _, values) in zip(exps, problems)
    ]
    return peaks, totals, outs


def lanes_of(columns):
    _, j = grid_ij((columns[0].shape[0], 128))
    block = jnp.zeros((columns[0].shape[0], 128), FULL)
    for lane, column in enumerate(columns):
        block = jnp.where(j == lane, column, block)
    return block


def near_kernel(q_ref, *refs):
    k_refs, v_refs, (out_ref, stat_ref) = refs[:4], refs[4:8], refs[8:]
    parts = heads_of(0, 5)
    peaks, totals, outs = softmax_all(
        [(q_ref[:, c], [k[:, c] for k in k_refs], [v[:, c] for v in v_refs]) for _, c in parts]
    )
    for (_, c), out, total in zip(parts, outs, totals):
        out_ref[:, c] = out * (1.0 / total)
    block = lanes_of([peak + jnp.log2(total) for peak, total in zip(peaks, totals)])
    stat_ref[0] = block.T[0:8]


def joined(refs, rows, c):
    return jnp.concatenate([r[:, :, rows, c].reshape(256, HD) for r in refs], 0)


def group_rows(a_ref, b_ref, y_ref, c):
    one = {
        "k": a_ref[0, :, 0:32, c], "v": a_ref[0, :, 32:64, c],
        "q": b_ref[0, :, 0:32, c], "g": b_ref[0, :, 32:64, c],
    }
    one = {name: x.reshape(128, HD) for name, x in one.items()}
    two = {name: y_ref[0, t, 0:16, c] for t, name in enumerate("kvqg")}
    return one, two


def group_forward_kernel(zs_ref, *refs):
    a0, a1, (y0, y1, ret_ref) = refs[0:2], refs[2:4], refs[4:]
    problems = []
    parts = heads_of(0, 3)
    for _, c in parts:
        q1 = zs_ref[:, 80:112, c].reshape(128, HD)
        problems.append((
            q1,
            [joined(r, slice(0, 32), c) for r in (a0, a1)],
            [joined(r, slice(32, 64), c) for r in (a0, a1)],
        ))
        problems.append((
            y0[0, 2, 0:16, c],
            [y[:, 0, :, c].reshape(256, HD) for y in (y0, y1)],
            [y[:, 1, :, c].reshape(256, HD) for y in (y0, y1)],
        ))
    peaks, totals, outs = softmax_all(problems)
    outs = [out * (1.0 / total) for out, total in zip(outs, totals)]
    lses = [peak + jnp.log2(total) for peak, total in zip(peaks, totals)]
    one, two = lanes_of(lses[0::2]), lanes_of(lses[1::2])
    for m in range(4):
        for (_, c), out1, out2 in zip(parts, outs[0::2], outs[1::2]):
            ret_ref[m, 0:32, c] = out1[32 * m : 32 * m + 32]
            ret_ref[m, 32:36, c] = out2[4 * m : 4 * m + 4]
        ret_ref[m, 0:32, 384:512] = one[32 * m : 32 * m + 32]
        ret_ref[m, 32:36, 384:512] = two[4 * m : 4 * m + 4]
        ret_ref[m, 36:40, :] = jnp.zeros((4, 512), FULL)


def thirds_of(x):
    pieces = []
    for _ in range(3):
        pieces.append(x.astype(HALF))
        x = x - pieces[-1].astype(FULL)
    return pieces


def row_times(row, onehot):
    i, _ = grid_ij((8, row.shape[1]))
    rows = jnp.zeros((8, row.shape[1]), FULL)
    for n, piece in enumerate(thirds_of(row)):
        rows = jnp.where(i == n, piece.astype(FULL), rows)
    return jnp.sum(dot_nn(rows.astype(HALF), onehot), 0, keepdims=True)


def transposed(rows):
    rows = list(rows)
    width = rows[0].shape[1]
    return jnp.concatenate(rows + [jnp.zeros((128 - len(rows), width), FULL)], 0).T


def merge_kernel(
    off_ref, near_ref, near_stat_ref, g_ref, ret_ref, att_ref, stat_ref, row_ref, sel_ref
):
    lses, scales, picked, far_scales, hits = [], [], [], [], []
    for h in range(H):
        mine = h // 3
        i, p = grid_ij((40, ROWS))
        one = (i < 32) & (p == 8 * i + off_ref[1, h])
        two = (i >= 32) & (i < 36) & (p == 64 * (i - 32) + off_ref[2, h])
        far = ret_ref[mine, :, 384:512].T[h % 3 : h % 3 + 1]
        both = row_times(far, jnp.concatenate([one, two], 1).astype(HALF))
        _, p = grid_ij((1, ROWS))
        lse0 = near_stat_ref[h // 5, h % 5 : h % 5 + 1, :]
        lse1 = jnp.where((p & 7) == off_ref[1, h], both[:, :ROWS], NEG)
        lse2 = jnp.where((p & 63) == off_ref[2, h], both[:, ROWS:], NEG)
        peak = jnp.maximum(jnp.maximum(lse0, lse1), lse2)
        total = jnp.exp2(lse0 - peak) + jnp.exp2(lse1 - peak) + jnp.exp2(lse2 - peak)
        lses.append(peak + jnp.log2(total))
        scales.append(jnp.exp2(lse0 - lses[-1]))
        p, j = grid_ij((ROWS, 128))
        target = jnp.where(j < 32, 8 * j + off_ref[1, h], 64 * (j - 32) + off_ref[2, h])
        hits.append(((p == target) & (j < 36)).astype(HALF))
        picked.append(row_times(lses[-1], hits[-1]))
        _, j = grid_ij((1, 40))
        far_scale = jnp.where(j < 36, jnp.exp2(jnp.minimum(far - picked[-1][:, :40], 1.0)), 0.0)
        far_scales.append(jnp.concatenate([far_scale, jnp.zeros((1, 88), FULL)], 1))
    scales = transposed(scales)
    far_scales = transposed(far_scales)
    dots = []
    for h, c in heads_of(0, H):
        mine, lane = h // 3, slice(h % 3 * HD, (h % 3 + 1) * HD)
        far = ret_ref[mine, :, lane] * far_scales[:40, h : h + 1]
        high = far.astype(HALF)
        low = (far - high.astype(FULL)).astype(HALF)
        lifted = dot_nn(hits[h][:, :40], jnp.concatenate([high, low], 1))
        out = near_ref[:, c] * scales[:, h : h + 1] + lifted[:, :HD] + lifted[:, HD:]
        att_ref[:, c] = out.astype(HALF)
        dots.append(jnp.sum(out * g_ref[:, c].astype(FULL), 1, keepdims=True))
    dots = lanes_of(dots).T
    dots = [dots[h : h + 1] for h in range(H)]
    for s in range(2):
        stat_ref[s] = transposed(lses[5 * s : 5 * s + 5] + dots[5 * s : 5 * s + 5])
    for s in range(5):
        rows = lses[2 * s : 2 * s + 2] + dots[2 * s : 2 * s + 2]
        row_ref[s] = jnp.concatenate(rows + [jnp.zeros((4, ROWS), FULL)], 0)
    picked += [jnp.zeros((1, 128), FULL)] * 2
    dots = [row_times(dots[h], hits[h]) for h in range(H)] + [jnp.zeros((1, 128), FULL)] * 2
    packed = jnp.zeros((8, 128), FULL)
    for j in range(3):
        rows = jnp.concatenate(picked[j::3] + dots[j::3], 0)
        packed = packed + (pltpu.roll(rows, 40 * j, 1) if j else rows)
    for z in range(4):
        block = jnp.concatenate([packed[z : z + 1], packed[4 + z : 5 + z]], 0)
        for i in range(32):
            sel_ref[i // 8 * 32 + 8 * z + i % 8] = block


def gradients(problems):
    probs = [jnp.exp2(dot_nt(a, b) * FACTOR - lse) for a, b, _, _, lse, _ in problems]
    dprobs = [dot_nt(c, d) for _, _, c, d, _, _ in problems]
    return [
        (prob.astype(HALF), (prob * (dprob - row_dot)).astype(HALF))
        for prob, dprob, (_, _, _, _, _, row_dot) in zip(probs, dprobs, problems)
    ]


def near_query_kernel(q_ref, g_ref, stat_ref, *refs):
    k_refs, v_refs, (dq_ref,) = refs[:4], refs[4:8], refs[8:]
    problems = []
    for part, (_, c) in enumerate(heads_of(0, 5)):
        lse = stat_ref[0, :, part : part + 1]
        row_dot = stat_ref[0, :, part + 5 : part + 6]
        for k, v in zip(k_refs, v_refs):
            problems.append((q_ref[:, c], k[:, c], g_ref[:, c], v[:, c], lse, row_dot))
    done = gradients(problems)
    for part, (_, c) in enumerate(heads_of(0, 5)):
        dq_ref[:, c] = sum(dot_nn(ds, k[:, c]) for (_, ds), k in zip(done[4 * part :], k_refs))


def gathered_stats(s_ref, c):
    _, lane = grid_ij((2, 128))
    one = [[], [], []]
    two = [[jnp.zeros((2, 128), FULL)] * 2 for _ in range(3)]

    def moved(rows, distance):
        return pltpu.roll(rows, distance % 128, 1) if distance % 128 else rows

    for y in range(4):
        for x, x_mask in enumerate(MASKS4):
            blocks = [jnp.zeros((2, 128), FULL)] * 3
            for z in range(4):
                source = (lax.axis_index("seqhi") ^ y) * 32 + (
                    8 * z + ((lax.axis_index("seqlo") & 7) ^ (2 * x_mask + c))
                )
                rows = s_ref[source]
                start = 64 * (y % 2) + 16 * x + 4 * z
                for j in range(3):
                    if y == 0:
                        blocks[j] = jnp.where(lane // 32 == z, moved(rows, 32 * z - 40 * j), blocks[j])
                    two[j][y // 2] = jnp.where(
                        (lane >= start) & (lane < start + 4),
                        moved(rows, start - 32 - 40 * j),
                        two[j][y // 2],
                    )
            if y == 0:
                for j in range(3):
                    one[j].append(blocks[j])
    return [jnp.concatenate(x, 1) for x in one], [jnp.concatenate(x, 1) for x in two]


def group_backward_kernel(*refs):
    a0, a1, b0, b1 = refs[0:2], refs[2:4], refs[4:6], refs[6:8]
    y0, y1, s_ref, out_ref = refs[8:]
    problems, others = [], []
    parts = heads_of(0, 3)
    s10, s20 = gathered_stats(s_ref, 0)
    s11, s21 = gathered_stats(s_ref, 1)
    for j, c in parts:
        one, two = group_rows(a0[0], b0[0], y0, c)
        sides = []
        for a, b, s in ((a0, b0, s10), (a1, b1, s11)):
            sides.append((
                joined(a, slice(0, 32), c), joined(a, slice(32, 64), c),
                joined(b, slice(0, 32), c), joined(b, slice(32, 64), c),
                s[j][0:1], s[j][1:2],
            ))
        for y, s in ((y0, s20), (y1, s21)):
            sides.append(
                tuple(y[:, t, :, c].reshape(256, HD) for t in range(4))
                + (s[j][0:1], s[j][1:2]))
        own = (one, one, two, two)
        for rows, n, (k, v, q, g, lse, row_dot) in zip(own, (128, 128, 16, 16), sides):
            first = sides[0] if n == 128 else sides[2]
            lse_own = eye_column(first[4][:, :n], n)
            dot_own = eye_column(first[5][:, :n], n)
            problems.append((rows["q"], k, rows["g"], v, lse_own, dot_own))
            others.append(k)
            problems.append((rows["k"], q, rows["v"], g, lse, row_dot))
            others.append((q, g))
    done = gradients(problems)
    for j, c in parts:
        mine, rest = done[8 * j : 8 * j + 8], others[8 * j : 8 * j + 8]
        dq = [dot_nn(mine[n][1], rest[n]) * SCALING for n in (0, 2, 4, 6)]
        dk = [dot_nn(mine[n][1], rest[n][0]) * SCALING for n in (1, 3, 5, 7)]
        dv = [dot_nn(mine[n][0], rest[n][1]) for n in (1, 3, 5, 7)]
        one = [(x[0] + x[1]).astype(HALF) for x in (dq, dk, dv)]
        two = [x[2] + x[3] for x in (dq, dk, dv)]
        for m in range(4):
            for t in range(3):
                out_ref[m, 32 * t : 32 * t + 32, c] = one[t][32 * m : 32 * m + 32]
            small = [x[4 * m : 4 * m + 4] for x in two] + [jnp.zeros((4, HD), FULL)]
            out_ref[m, 96:112, c] = jnp.concatenate(small, 0).astype(HALF)


def near_key_kernel(k_ref, v_ref, *refs):
    qg_refs, s_refs, (dk_ref, dv_ref) = refs[:4], refs[4:8], refs[8:]
    problems = []
    for part, (_, c) in enumerate(heads_of(0)):
        for qg, s in zip(qg_refs, s_refs):
            lse, row_dot = s[0, part : part + 1, :], s[0, part + 2 : part + 3, :]
            problems.append((k_ref[:, c], qg[0, :, c], v_ref[:, c], qg[1, :, c], lse, row_dot))
    done = gradients(problems)
    for part, (_, c) in enumerate(heads_of(0)):
        mine = done[4 * part : 4 * part + 4]
        dk_ref[:, c] = sum(dot_nn(ds, qg[0, :, c]) for (_, ds), qg in zip(mine, qg_refs))
        dv_ref[:, c] = sum(dot_nn(prob, qg[1, :, c]) for (prob, _), qg in zip(mine, qg_refs))


def add_kernel(
    off_ref, dq_near_ref, dk_near_ref, dv_near_ref, back_ref, dq_ref, dk_ref, dv_ref
):
    p, r = grid_ij((ROWS, 112))
    tensor = jnp.where(r < 96, r // 32, (r - 96) // 4)
    for h, c in heads_of(pl.program_id(0), 5):
        target = jnp.where(r < 96, 8 * (r & 31) + off_ref[1, h], 64 * (r & 3) + off_ref[2, h])
        hit = p == target
        rows = back_ref[h // 3, :, pl.ds(pl.multiple_of(h % 3 * HD, HD), HD)]
        lifted = [dot_nn((hit & (tensor == t)).astype(HALF), rows) for t in range(3)]
        dq_ref[:, c] = (dq_near_ref[:, c] * SCALING + lifted[0]).astype(HALF)
        dk_ref[:, c] = (dk_near_ref[:, c] * SCALING + lifted[1]).astype(HALF)
        dv_ref[:, c] = (dv_near_ref[:, c] + lifted[2]).astype(HALF)


COLUMNS = pl.BlockSpec((ROWS, 2 * HD), lambda s, *_: (0, s))
PAIR = pl.BlockSpec((2, ROWS, 2 * HD), lambda s, *_: (0, 0, s))
FIVE = pl.BlockSpec((ROWS, 5 * HD), lambda s, *_: (0, s))
LANES = pl.BlockSpec((1, ROWS, 128), lambda s, *_: (s, 0, 0))
STAT_ROWS = pl.BlockSpec((1, 8, ROWS), lambda s, *_: (s, 0, 0))


def whole(*shape):
    return pl.BlockSpec(shape, lambda *_: (0,) * len(shape))


def array(*shape, dtype=HALF):
    return jax.ShapeDtypeStruct(shape, dtype)


def call(kernel, name, steps, in_specs, out_specs, out_shape, operands, prefetch=0, room=60, time=0.001):
    return pl.pallas_call(
        kernel,
        grid_spec=pltpu.PrefetchScalarGridSpec(
            num_scalar_prefetch=prefetch, grid=(steps,), in_specs=in_specs, out_specs=out_specs
        ),
        out_shape=out_shape,
        compiler_params=pltpu.CompilerParams(vmem_limit_bytes=room * 1024 * 1024),
        cost_estimate=pl.CostEstimate(flops=int(time * 1_150_000_000), bytes_accessed=100_000, transcendentals=0),
        name=name,
    )(*operands)


CORE, X1, X3 = 1, 2, 6
MASKS4 = (0, 1, 3, 2)
ZS = (8, 16, 24)


def two_steps(x, axis, first, second):
    x = jnp.stack([x, swapped(x, axis, first)])
    return jnp.concatenate([x, swapped(x, axis, second)], 0)


def around(x, axis, masks):
    return [x] + [swapped(x, axis, m) for m in masks]


def over_z(parts):
    groups = [[8 * z + i for z in range(4)] for i in range(8)]
    return lax.all_to_all(parts, "seqlo", 0, 0, axis_index_groups=groups, tiled=True)


def core(x):
    return swapped(x, "seqlo", CORE)


def body(query, key, value, grad_out, offsets):
    kx = swapped(key, "seqlo", X1)
    zs = call(
        pick_kernel, "pick_rows", 1, [whole(*WIDE)] * 4, [whole(4, 144, 384)],
        [array(4, 144, 384)], (offsets, key, value, query, grad_out), prefetch=1,
    )[0]
    zs = over_z(zs)
    a, y, b, kx = together(zs[:, :64], zs[:, 64:80], zs[:, 80:], kx)
    y = jnp.stack([y, swapped(y, "seqlo", X1)])
    a, y, b = together(a, y, b)
    a, b = [jnp.stack([t, swapped(t, "seqlo", X1)]) for t in (a, b)]
    y = jnp.concatenate([y, swapped(y, "seqlo", X3)], 0)
    value_out, a, b, y = together(value, a, b, y)
    vx = swapped(value_out, "seqlo", X1)
    a3 = swapped(a, "seqlo", X3)
    y = y.reshape(4, 4, 4, 4, 384).transpose(2, 0, 1, 3, 4).reshape(4, 64, 384)
    y = around(y, "seqhi", (1, 2, 3))
    a3, *y = together(a3, *y)
    b3 = swapped(b, "seqlo", X3)
    both, vx = together(jnp.stack([query, grad_out]), vx)
    both_x = swapped(both, "seqlo", X1)
    y = jnp.stack(y)
    a, y = [a, a3, core(a), core(a3)], [y, core(y)]
    part_spec, y_spec = whole(2, 4, 64, 384), whole(4, 4, 64, 384)
    (ret,) = call(
        group_forward_kernel, "group_forward", 1,
        [whole(4, 144, 384)] + [part_spec] * 4 + [y_spec] * 2, [whole(4, 40, 512)],
        [array(4, 40, 512, dtype=FULL)], (zs, *a, *y),
    )
    near_query, ret = together(query, ret)
    ret = over_z(ret)
    keys0 = [key, core(key), kx, core(kx)]
    values0 = [value, core(value), vx, core(vx)]
    near, near_stat = call(
        near_kernel, "near_forward", 2, [FIVE] * 9, [FIVE, STAT_ROWS],
        [array(*WIDE, dtype=FULL), array(2, 8, ROWS, dtype=FULL)],
        (near_query, *keys0, *values0),
    )
    ret, near_stat, b3 = together(ret, near_stat, b3)
    attended, stat, rows, sel = call(
        merge_kernel, "merge_levels", 1,
        [whole(*WIDE), whole(2, 8, ROWS), whole(*WIDE), whole(4, 40, 512)],
        [whole(*WIDE), whole(2, ROWS, 128), whole(5, 8, ROWS), whole(128, 2, 128)],
        [
            array(*WIDE), array(2, ROWS, 128, dtype=FULL), array(5, 8, ROWS, dtype=FULL),
            array(128, 2, 128, dtype=FULL),
        ],
        (offsets, near, near_stat, grad_out, ret), prefetch=1,
    )

    sel = lax.all_to_all(sel, ("seqhi", "seqlo"), 0, 0, tiled=True)
    b = [b, b3, core(b), core(b3)]
    sx = swapped(rows, "seqlo", X1)
    stat, both_x = together(stat, both_x)
    both = [both, core(both), both_x, core(both_x)]
    (dq_near,) = call(
        near_query_kernel, "near_query_gradient", 2, [FIVE] * 2 + [LANES] + [FIVE] * 8,
        [FIVE], [array(*WIDE, dtype=FULL)],
        (query, grad_out, stat, *keys0, *values0), time=8,
    )
    sel, dq_near = together(sel, dq_near)
    (back,) = call(
        group_backward_kernel, "group_backward", 1,
        [part_spec] * 8 + [y_spec] * 2 + [whole(128, 2, 128)],
        [whole(4, 112, 384)], [array(4, 112, 384)],
        (*a, *b, *y, sel),
    )
    sx, back = together(sx, back)
    s0 = [rows, core(rows), sx, core(sx)]
    dk_near, dv_near = call(
        near_key_kernel, "near_key_gradient", 5, [COLUMNS] * 2 + [PAIR] * 4 + [STAT_ROWS] * 4, [COLUMNS] * 2,
        [array(*WIDE, dtype=FULL)] * 2, (key, value, *both, *s0),
    )
    back = over_z(back)
    back, dk_near = together(back, dk_near)
    grad_query, grad_key, grad_value = call(
        add_kernel, "add_levels", 2,
        [FIVE] * 3 + [whole(4, 112, 384)], [FIVE] * 3, [array(*WIDE)] * 3,
        (offsets, dq_near, dk_near, dv_near, back), prefetch=1,
    )
    return attended, grad_query, grad_key, grad_value


def solution(mesh):
    spec = P(("seqhi", "seqlo"), None)
    return jax.shard_map(
        body,
        mesh=mesh,
        in_specs=(spec, spec, spec, spec, P()),
        out_specs=(spec, spec, spec, spec),
        check_vma=False,
    )
```

```python
import functools

import jax
import jax.numpy as jnp
from jax import lax
from jax.experimental import pallas as pl
from jax.experimental.pallas import tpu as pltpu
from jax.sharding import PartitionSpec as P

H = 10
HD = 128
ROWS = 256
SCALING = HD ** -0.5
LOG2E = 1.4426950408889634
FACTOR = SCALING * LOG2E
NEG = -1e30
WIDE = (ROWS, H * HD)
HALF = jnp.bfloat16
FULL = jnp.float32


def swapped(x, axis, mask):
    return lax.ppermute(x, axis, [(i, i ^ mask) for i in range(lax.axis_size(axis))])


def together(*arrays):
    return lax.optimization_barrier(arrays)


def dot_nt(a, b):
    return lax.dot_general(a, b, (((1,), (1,)), ((), ())), preferred_element_type=FULL)


def dot_nn(a, b):
    return lax.dot_general(a, b, (((1,), (0,)), ((), ())), preferred_element_type=FULL)


def grid_ij(shape):
    return (
        lax.broadcasted_iota(jnp.int32, shape, 0),
        lax.broadcasted_iota(jnp.int32, shape, 1),
    )


def eye_column(row, n):
    i, j = grid_ij((n, n))
    return jnp.sum(jnp.where(i == j, row, 0.0), 1, keepdims=True)


def heads_of(step, parts=2):
    return [(step * parts + part, slice(part * HD, (part + 1) * HD)) for part in range(parts)]


def pick_kernel(off_ref, k_ref, v_ref, q_ref, g_ref, out_ref):
    i, p = grid_ij((48, ROWS))
    out_ref[3, :, HD:] = jnp.zeros((144, 2 * HD), HALF)
    for h, lanes in heads_of(0, H):
        z, cols = h // 3, slice(h % 3 * HD, (h % 3 + 1) * HD)
        one = (i < 32) & (p == 8 * i + off_ref[1, h])
        two = (i >= 32) & (p == 64 * (i & 3) + off_ref[2, h])
        rows = [
            dot_nn((one | (two & ((i - 32) // 4 == t))).astype(HALF), r[:, lanes])
            for t, r in enumerate((k_ref, v_ref, q_ref, g_ref))
        ]
        out_ref[z, 0:32, cols] = rows[0][:32].astype(HALF)
        out_ref[z, 32:64, cols] = rows[1][:32].astype(HALF)
        out_ref[z, 64:80, cols] = sum(x[32:] for x in rows).astype(HALF)
        out_ref[z, 80:112, cols] = rows[2][:32].astype(HALF)
        out_ref[z, 112:144, cols] = rows[3][:32].astype(HALF)


def softmax_all(problems):
    scores = [[dot_nt(q, k) * FACTOR for k in keys] for q, keys, _ in problems]
    peaks = [
        functools.reduce(jnp.maximum, [jnp.max(s, 1, keepdims=True) for s in part])
        for part in scores
    ]
    exps = [[jnp.exp2(s - peak) for s in part] for part, peak in zip(scores, peaks)]
    totals = [sum(jnp.sum(e, 1, keepdims=True) for e in part) for part in exps]
    outs = [
        sum(dot_nn(e.astype(HALF), v) for e, v in zip(part, values))
        for part, (_, _, values) in zip(exps, problems)
    ]
    return peaks, totals, outs


def lanes_of(columns):
    _, j = grid_ij((columns[0].shape[0], 128))
    block = jnp.zeros((columns[0].shape[0], 128), FULL)
    for lane, column in enumerate(columns):
        block = jnp.where(j == lane, column, block)
    return block


def near_kernel(q_ref, *refs):
    k_refs, v_refs, (out_ref, stat_ref) = refs[:4], refs[4:8], refs[8:]
    parts = heads_of(0, 5)
    peaks, totals, outs = softmax_all(
        [(q_ref[:, c], [k[:, c] for k in k_refs], [v[:, c] for v in v_refs]) for _, c in parts]
    )
    for (_, c), out, total in zip(parts, outs, totals):
        out_ref[:, c] = out * (1.0 / total)
    block = lanes_of([peak + jnp.log2(total) for peak, total in zip(peaks, totals)])
    stat_ref[0] = block.T[0:8]


def joined(refs, rows, c):
    return jnp.concatenate([r[:, :, rows, c].reshape(256, HD) for r in refs], 0)


def group_rows(a_ref, b_ref, y_ref, c):
    one = {
        "k": a_ref[0, :, 0:32, c], "v": a_ref[0, :, 32:64, c],
        "q": b_ref[0, :, 0:32, c], "g": b_ref[0, :, 32:64, c],
    }
    one = {name: x.reshape(128, HD) for name, x in one.items()}
    two = {name: y_ref[0, t, 0:16, c] for t, name in enumerate("kvqg")}
    return one, two


def group_forward_kernel(zs_ref, *refs):
    a0, a1, (y0, y1, ret_ref) = refs[0:2], refs[2:4], refs[4:]
    problems = []
    parts = heads_of(0, 3)
    for _, c in parts:
        q1 = zs_ref[:, 80:112, c].reshape(128, HD)
        problems.append((
            q1,
            [joined(r, slice(0, 32), c) for r in (a0, a1)],
            [joined(r, slice(32, 64), c) for r in (a0, a1)],
        ))
        problems.append((
            y0[0, 2, 0:16, c],
            [y[:, 0, :, c].reshape(256, HD) for y in (y0, y1)],
            [y[:, 1, :, c].reshape(256, HD) for y in (y0, y1)],
        ))
    peaks, totals, outs = softmax_all(problems)
    outs = [out * (1.0 / total) for out, total in zip(outs, totals)]
    lses = [peak + jnp.log2(total) for peak, total in zip(peaks, totals)]
    one, two = lanes_of(lses[0::2]), lanes_of(lses[1::2])
    for m in range(4):
        for (_, c), out1, out2 in zip(parts, outs[0::2], outs[1::2]):
            ret_ref[m, 0:32, c] = out1[32 * m : 32 * m + 32]
            ret_ref[m, 32:36, c] = out2[4 * m : 4 * m + 4]
        ret_ref[m, 0:32, 384:512] = one[32 * m : 32 * m + 32]
        ret_ref[m, 32:36, 384:512] = two[4 * m : 4 * m + 4]
        ret_ref[m, 36:40, :] = jnp.zeros((4, 512), FULL)


def thirds_of(x):
    pieces = []
    for _ in range(3):
        pieces.append(x.astype(HALF))
        x = x - pieces[-1].astype(FULL)
    return pieces


def row_times(row, onehot):
    i, _ = grid_ij((8, row.shape[1]))
    rows = jnp.zeros((8, row.shape[1]), FULL)
    for n, piece in enumerate(thirds_of(row)):
        rows = jnp.where(i == n, piece.astype(FULL), rows)
    return jnp.sum(dot_nn(rows.astype(HALF), onehot), 0, keepdims=True)


def transposed(rows):
    rows = list(rows)
    width = rows[0].shape[1]
    return jnp.concatenate(rows + [jnp.zeros((128 - len(rows), width), FULL)], 0).T


def merge_kernel(
    off_ref, near_ref, near_stat_ref, g_ref, ret_ref, att_ref, stat_ref, row_ref, sel_ref
):
    lses, scales, picked, far_scales, hits = [], [], [], [], []
    for h in range(H):
        mine = h // 3
        i, p = grid_ij((40, ROWS))
        one = (i < 32) & (p == 8 * i + off_ref[1, h])
        two = (i >= 32) & (i < 36) & (p == 64 * (i - 32) + off_ref[2, h])
        far = ret_ref[mine, :, 384:512].T[h % 3 : h % 3 + 1]
        both = row_times(far, jnp.concatenate([one, two], 1).astype(HALF))
        _, p = grid_ij((1, ROWS))
        lse0 = near_stat_ref[h // 5, h % 5 : h % 5 + 1, :]
        lse1 = jnp.where((p & 7) == off_ref[1, h], both[:, :ROWS], NEG)
        lse2 = jnp.where((p & 63) == off_ref[2, h], both[:, ROWS:], NEG)
        peak = jnp.maximum(jnp.maximum(lse0, lse1), lse2)
        total = jnp.exp2(lse0 - peak) + jnp.exp2(lse1 - peak) + jnp.exp2(lse2 - peak)
        lses.append(peak + jnp.log2(total))
        scales.append(jnp.exp2(lse0 - lses[-1]))
        p, j = grid_ij((ROWS, 128))
        target = jnp.where(j < 32, 8 * j + off_ref[1, h], 64 * (j - 32) + off_ref[2, h])
        hits.append(((p == target) & (j < 36)).astype(HALF))
        picked.append(row_times(lses[-1], hits[-1]))
        _, j = grid_ij((1, 40))
        far_scale = jnp.where(j < 36, jnp.exp2(jnp.minimum(far - picked[-1][:, :40], 1.0)), 0.0)
        far_scales.append(jnp.concatenate([far_scale, jnp.zeros((1, 88), FULL)], 1))
    scales = transposed(scales)
    far_scales = transposed(far_scales)
    dots = []
    for h, c in heads_of(0, H):
        mine, lane = h // 3, slice(h % 3 * HD, (h % 3 + 1) * HD)
        far = ret_ref[mine, :, lane] * far_scales[:40, h : h + 1]
        high = far.astype(HALF)
        low = (far - high.astype(FULL)).astype(HALF)
        lifted = dot_nn(hits[h][:, :40], jnp.concatenate([high, low], 1))
        out = near_ref[:, c] * scales[:, h : h + 1] + lifted[:, :HD] + lifted[:, HD:]
        att_ref[:, c] = out.astype(HALF)
        dots.append(jnp.sum(out * g_ref[:, c].astype(FULL), 1, keepdims=True))
    dots = lanes_of(dots).T
    dots = [dots[h : h + 1] for h in range(H)]
    for s in range(2):
        stat_ref[s] = transposed(lses[5 * s : 5 * s + 5] + dots[5 * s : 5 * s + 5])
    for s in range(5):
        rows = lses[2 * s : 2 * s + 2] + dots[2 * s : 2 * s + 2]
        row_ref[s] = jnp.concatenate(rows + [jnp.zeros((4, ROWS), FULL)], 0)
    picked += [jnp.zeros((1, 128), FULL)] * 2
    dots = [row_times(dots[h], hits[h]) for h in range(H)] + [jnp.zeros((1, 128), FULL)] * 2
    packed = jnp.zeros((8, 128), FULL)
    for j in range(3):
        rows = jnp.concatenate(picked[j::3] + dots[j::3], 0)
        packed = packed + (pltpu.roll(rows, 40 * j, 1) if j else rows)
    for z in range(4):
        block = jnp.concatenate([packed[z : z + 1], packed[4 + z : 5 + z]], 0)
        for i in range(32):
            sel_ref[i // 8 * 32 + 8 * z + i % 8] = block


def gradients(problems):
    probs = [jnp.exp2(dot_nt(a, b) * FACTOR - lse) for a, b, _, _, lse, _ in problems]
    dprobs = [dot_nt(c, d) for _, _, c, d, _, _ in problems]
    return [
        (prob.astype(HALF), (prob * (dprob - row_dot)).astype(HALF))
        for prob, dprob, (_, _, _, _, _, row_dot) in zip(probs, dprobs, problems)
    ]


def near_query_kernel(q_ref, g_ref, stat_ref, *refs):
    k_refs, v_refs, (dq_ref,) = refs[:4], refs[4:8], refs[8:]
    problems = []
    for part, (_, c) in enumerate(heads_of(0, 5)):
        lse = stat_ref[0, :, part : part + 1]
        row_dot = stat_ref[0, :, part + 5 : part + 6]
        for k, v in zip(k_refs, v_refs):
            problems.append((q_ref[:, c], k[:, c], g_ref[:, c], v[:, c], lse, row_dot))
    done = gradients(problems)
    for part, (_, c) in enumerate(heads_of(0, 5)):
        dq = sum(dot_nn(ds, k[:, c]) for (_, ds), k in zip(done[4 * part :], k_refs))
        dq_ref[:, c] = dq.astype(HALF)


def gathered_stats(s_ref, c):
    _, lane = grid_ij((2, 128))
    one = [[], [], []]
    two = [[jnp.zeros((2, 128), FULL)] * 2 for _ in range(3)]

    def moved(rows, distance):
        return pltpu.roll(rows, distance % 128, 1) if distance % 128 else rows

    for y in range(4):
        for x, x_mask in enumerate(MASKS4):
            blocks = [jnp.zeros((2, 128), FULL)] * 3
            for z in range(4):
                source = (lax.axis_index("seqhi") ^ y) * 32 + (
                    8 * z + ((lax.axis_index("seqlo") & 7) ^ (2 * x_mask + c))
                )
                rows = s_ref[source]
                start = 64 * (y % 2) + 16 * x + 4 * z
                for j in range(3):
                    if y == 0:
                        blocks[j] = jnp.where(lane // 32 == z, moved(rows, 32 * z - 40 * j), blocks[j])
                    two[j][y // 2] = jnp.where(
                        (lane >= start) & (lane < start + 4),
                        moved(rows, start - 32 - 40 * j),
                        two[j][y // 2],
                    )
            if y == 0:
                for j in range(3):
                    one[j].append(blocks[j])
    return [jnp.concatenate(x, 1) for x in one], [jnp.concatenate(x, 1) for x in two]


def group_backward_kernel(*refs):
    a0, a1, b0, b1 = refs[0:2], refs[2:4], refs[4:6], refs[6:8]
    y0, y1, s_ref, out_ref = refs[8:]
    problems, others = [], []
    parts = heads_of(0, 3)
    s10, s20 = gathered_stats(s_ref, 0)
    s11, s21 = gathered_stats(s_ref, 1)
    for j, c in parts:
        one, two = group_rows(a0[0], b0[0], y0, c)
        sides = []
        for a, b, s in ((a0, b0, s10), (a1, b1, s11)):
            sides.append((
                joined(a, slice(0, 32), c), joined(a, slice(32, 64), c),
                joined(b, slice(0, 32), c), joined(b, slice(32, 64), c),
                s[j][0:1], s[j][1:2],
            ))
        for y, s in ((y0, s20), (y1, s21)):
            sides.append(
                tuple(y[:, t, :, c].reshape(256, HD) for t in range(4))
                + (s[j][0:1], s[j][1:2]))
        own = (one, one, two, two)
        for rows, n, (k, v, q, g, lse, row_dot) in zip(own, (128, 128, 16, 16), sides):
            first = sides[0] if n == 128 else sides[2]
            lse_own = eye_column(first[4][:, :n], n)
            dot_own = eye_column(first[5][:, :n], n)
            problems.append((rows["q"], k, rows["g"], v, lse_own, dot_own))
            others.append(k)
            problems.append((rows["k"], q, rows["v"], g, lse, row_dot))
            others.append((q, g))
    done = gradients(problems)
    for j, c in parts:
        mine, rest = done[8 * j : 8 * j + 8], others[8 * j : 8 * j + 8]
        dq = [dot_nn(mine[n][1], rest[n]) * SCALING for n in (0, 2, 4, 6)]
        dk = [dot_nn(mine[n][1], rest[n][0]) * SCALING for n in (1, 3, 5, 7)]
        dv = [dot_nn(mine[n][0], rest[n][1]) for n in (1, 3, 5, 7)]
        one = [(x[0] + x[1]).astype(HALF) for x in (dq, dk, dv)]
        two = [x[2] + x[3] for x in (dq, dk, dv)]
        for m in range(4):
            for t in range(3):
                out_ref[m, 32 * t : 32 * t + 32, c] = one[t][32 * m : 32 * m + 32]
            small = [x[4 * m : 4 * m + 4] for x in two] + [jnp.zeros((4, HD), FULL)]
            out_ref[m, 96:112, c] = jnp.concatenate(small, 0).astype(HALF)


def near_key_kernel(k_ref, v_ref, *refs):
    qg_refs, s_refs, (dk_ref, dv_ref) = refs[:4], refs[4:8], refs[8:]
    problems = []
    for part, (_, c) in enumerate(heads_of(0)):
        for qg, s in zip(qg_refs, s_refs):
            lse, row_dot = s[0, part : part + 1, :], s[0, part + 2 : part + 3, :]
            problems.append((k_ref[:, c], qg[0, :, c], v_ref[:, c], qg[1, :, c], lse, row_dot))
    done = gradients(problems)
    for part, (_, c) in enumerate(heads_of(0)):
        mine = done[4 * part : 4 * part + 4]
        dk = sum(dot_nn(ds, qg[0, :, c]) for (_, ds), qg in zip(mine, qg_refs))
        dk_ref[:, c] = dk.astype(HALF)
        dv = sum(dot_nn(prob, qg[1, :, c]) for (prob, _), qg in zip(mine, qg_refs))
        dv_ref[:, c] = dv.astype(HALF)


def add_kernel(
    off_ref, dq_near_ref, dk_near_ref, dv_near_ref, back_ref, dq_ref, dk_ref, dv_ref
):
    p, r = grid_ij((ROWS, 112))
    tensor = jnp.where(r < 96, r // 32, (r - 96) // 4)
    for h, c in heads_of(pl.program_id(0), 5):
        target = jnp.where(r < 96, 8 * (r & 31) + off_ref[1, h], 64 * (r & 3) + off_ref[2, h])
        hit = p == target
        rows = back_ref[h // 3, :, pl.ds(pl.multiple_of(h % 3 * HD, HD), HD)]
        lifted = [dot_nn((hit & (tensor == t)).astype(HALF), rows) for t in range(3)]
        dq_ref[:, c] = (dq_near_ref[:, c].astype(FULL) * SCALING + lifted[0]).astype(HALF)
        dk_ref[:, c] = (dk_near_ref[:, c].astype(FULL) * SCALING + lifted[1]).astype(HALF)
        dv_ref[:, c] = (dv_near_ref[:, c].astype(FULL) + lifted[2]).astype(HALF)


COLUMNS = pl.BlockSpec((ROWS, 2 * HD), lambda s, *_: (0, s))
PAIR = pl.BlockSpec((2, ROWS, 2 * HD), lambda s, *_: (0, 0, s))
FIVE = pl.BlockSpec((ROWS, 5 * HD), lambda s, *_: (0, s))
LANES = pl.BlockSpec((1, ROWS, 128), lambda s, *_: (s, 0, 0))
STAT_ROWS = pl.BlockSpec((1, 8, ROWS), lambda s, *_: (s, 0, 0))


def whole(*shape):
    return pl.BlockSpec(shape, lambda *_: (0,) * len(shape))


def array(*shape, dtype=HALF):
    return jax.ShapeDtypeStruct(shape, dtype)


def call(kernel, name, steps, in_specs, out_specs, out_shape, operands, prefetch=0, room=60, time=0.001):
    return pl.pallas_call(
        kernel,
        grid_spec=pltpu.PrefetchScalarGridSpec(
            num_scalar_prefetch=prefetch, grid=(steps,), in_specs=in_specs, out_specs=out_specs
        ),
        out_shape=out_shape,
        compiler_params=pltpu.CompilerParams(vmem_limit_bytes=room * 1024 * 1024),
        cost_estimate=pl.CostEstimate(flops=int(time * 1_150_000_000), bytes_accessed=100_000, transcendentals=0),
        name=name,
    )(*operands)


CORE, X1, X3 = 1, 2, 6
MASKS4 = (0, 1, 3, 2)
ZS = (8, 16, 24)


def two_steps(x, axis, first, second):
    x = jnp.stack([x, swapped(x, axis, first)])
    return jnp.concatenate([x, swapped(x, axis, second)], 0)


def around(x, axis, masks):
    return [x] + [swapped(x, axis, m) for m in masks]


def over_z(parts):
    groups = [[8 * z + i for z in range(4)] for i in range(8)]
    return lax.all_to_all(parts, "seqlo", 0, 0, axis_index_groups=groups, tiled=True)


def core(x):
    return swapped(x, "seqlo", CORE)


def body(query, key, value, grad_out, offsets):
    kx = swapped(key, "seqlo", X1)
    zs = call(
        pick_kernel, "pick_rows", 1, [whole(*WIDE)] * 4, [whole(4, 144, 384)],
        [array(4, 144, 384)], (offsets, key, value, query, grad_out), prefetch=1,
    )[0]
    zs = over_z(zs)
    a, y, b, kx = together(zs[:, :64], zs[:, 64:80], zs[:, 80:], kx)
    y = jnp.stack([y, swapped(y, "seqlo", X1)])
    a, y, b = together(a, y, b)
    a, b = [jnp.stack([t, swapped(t, "seqlo", X1)]) for t in (a, b)]
    y = jnp.concatenate([y, swapped(y, "seqlo", X3)], 0)
    value_out, a, b, y = together(value, a, b, y)
    vx = swapped(value_out, "seqlo", X1)
    a3 = swapped(a, "seqlo", X3)
    y = y.reshape(4, 4, 4, 4, 384).transpose(2, 0, 1, 3, 4).reshape(4, 64, 384)
    y = around(y, "seqhi", (1, 2, 3))
    a3, *y = together(a3, *y)
    b3 = swapped(b, "seqlo", X3)
    both, vx = together(jnp.stack([query, grad_out]), vx)
    both_x = swapped(both, "seqlo", X1)
    y = jnp.stack(y)
    a, y = [a, a3, core(a), core(a3)], [y, core(y)]
    part_spec, y_spec = whole(2, 4, 64, 384), whole(4, 4, 64, 384)
    (ret,) = call(
        group_forward_kernel, "group_forward", 1,
        [whole(4, 144, 384)] + [part_spec] * 4 + [y_spec] * 2, [whole(4, 40, 512)],
        [array(4, 40, 512, dtype=FULL)], (zs, *a, *y),
    )
    near_query, ret = together(query, ret)
    ret = over_z(ret)
    keys0 = [key, core(key), kx, core(kx)]
    values0 = [value, core(value), vx, core(vx)]
    near, near_stat = call(
        near_kernel, "near_forward", 2, [FIVE] * 9, [FIVE, STAT_ROWS],
        [array(*WIDE, dtype=FULL), array(2, 8, ROWS, dtype=FULL)],
        (near_query, *keys0, *values0),
    )
    ret, near_stat, b3 = together(ret, near_stat, b3)
    attended, stat, rows, sel = call(
        merge_kernel, "merge_levels", 1,
        [whole(*WIDE), whole(2, 8, ROWS), whole(*WIDE), whole(4, 40, 512)],
        [whole(*WIDE), whole(2, ROWS, 128), whole(5, 8, ROWS), whole(128, 2, 128)],
        [
            array(*WIDE), array(2, ROWS, 128, dtype=FULL), array(5, 8, ROWS, dtype=FULL),
            array(128, 2, 128, dtype=FULL),
        ],
        (offsets, near, near_stat, grad_out, ret), prefetch=1,
    )

    sel = lax.all_to_all(sel, ("seqhi", "seqlo"), 0, 0, tiled=True)
    b = [b, b3, core(b), core(b3)]
    sx = swapped(rows, "seqlo", X1)
    stat, both_x = together(stat, both_x)
    both = [both, core(both), both_x, core(both_x)]
    (dq_near,) = call(
        near_query_kernel, "near_query_gradient", 2, [FIVE] * 2 + [LANES] + [FIVE] * 8,
        [FIVE], [array(*WIDE)],
        (query, grad_out, stat, *keys0, *values0), time=8,
    )
    sel, dq_near = together(sel, dq_near)
    (back,) = call(
        group_backward_kernel, "group_backward", 1,
        [part_spec] * 8 + [y_spec] * 2 + [whole(128, 2, 128)],
        [whole(4, 112, 384)], [array(4, 112, 384)],
        (*a, *b, *y, sel),
    )
    sx, back = together(sx, back)
    s0 = [rows, core(rows), sx, core(sx)]
    dk_near, dv_near = call(
        near_key_kernel, "near_key_gradient", 5, [COLUMNS] * 2 + [PAIR] * 4 + [STAT_ROWS] * 4, [COLUMNS] * 2,
        [array(*WIDE)] * 2, (key, value, *both, *s0),
    )
    back = over_z(back)
    back, dk_near = together(back, dk_near)
    grad_query, grad_key, grad_value = call(
        add_kernel, "add_levels", 2,
        [FIVE] * 3 + [whole(4, 112, 384)], [FIVE] * 3, [array(*WIDE)] * 3,
        (offsets, dq_near, dk_near, dv_near, back), prefetch=1,
    )
    return attended, grad_query, grad_key, grad_value


def solution(mesh):
    spec = P(("seqhi", "seqlo"), None)
    return jax.shard_map(
        body,
        mesh=mesh,
        in_specs=(spec, spec, spec, spec, P()),
        out_specs=(spec, spec, spec, spec),
        check_vma=False,
    )
```

```python
import functools

import jax
import jax.numpy as jnp
from jax import lax
from jax.experimental import pallas as pl
from jax.experimental.pallas import tpu as pltpu
from jax.sharding import PartitionSpec as P

H = 10
HD = 128
ROWS = 256
SCALING = HD ** -0.5
LOG2E = 1.4426950408889634
FACTOR = SCALING * LOG2E
NEG = -1e30
WIDE = (ROWS, H * HD)
HALF = jnp.bfloat16
FULL = jnp.float32


def swapped(x, axis, mask):
    return lax.ppermute(x, axis, [(i, i ^ mask) for i in range(lax.axis_size(axis))])


def together(*arrays):
    return lax.optimization_barrier(arrays)


def dot_nt(a, b):
    return lax.dot_general(a, b, (((1,), (1,)), ((), ())), preferred_element_type=FULL)


def dot_nn(a, b):
    return lax.dot_general(a, b, (((1,), (0,)), ((), ())), preferred_element_type=FULL)


def grid_ij(shape):
    return (
        lax.broadcasted_iota(jnp.int32, shape, 0),
        lax.broadcasted_iota(jnp.int32, shape, 1),
    )


def eye_column(row, n):
    i, j = grid_ij((n, n))
    return jnp.sum(jnp.where(i == j, row, 0.0), 1, keepdims=True)


def heads_of(step, parts=2):
    return [(step * parts + part, slice(part * HD, (part + 1) * HD)) for part in range(parts)]


def pick_kernel(off_ref, k_ref, v_ref, q_ref, g_ref, out_ref):
    i, p = grid_ij((48, ROWS))
    out_ref[3, :, HD:] = jnp.zeros((144, 2 * HD), HALF)
    for h, lanes in heads_of(0, H):
        z, cols = h // 3, slice(h % 3 * HD, (h % 3 + 1) * HD)
        one = (i < 32) & (p == 8 * i + off_ref[1, h])
        two = (i >= 32) & (p == 64 * (i & 3) + off_ref[2, h])
        rows = [
            dot_nn((one | (two & ((i - 32) // 4 == t))).astype(HALF), r[:, lanes])
            for t, r in enumerate((k_ref, v_ref, q_ref, g_ref))
        ]
        out_ref[z, 0:32, cols] = rows[0][:32].astype(HALF)
        out_ref[z, 32:64, cols] = rows[1][:32].astype(HALF)
        out_ref[z, 64:80, cols] = sum(x[32:] for x in rows).astype(HALF)
        out_ref[z, 80:112, cols] = rows[2][:32].astype(HALF)
        out_ref[z, 112:144, cols] = rows[3][:32].astype(HALF)


def softmax_all(problems):
    scores = [[dot_nt(q, k) * FACTOR for k in keys] for q, keys, _ in problems]
    peaks = [
        functools.reduce(jnp.maximum, [jnp.max(s, 1, keepdims=True) for s in part])
        for part in scores
    ]
    exps = [[jnp.exp2(s - peak) for s in part] for part, peak in zip(scores, peaks)]
    totals = [sum(jnp.sum(e, 1, keepdims=True) for e in part) for part in exps]
    outs = [
        sum(dot_nn(e.astype(HALF), v) for e, v in zip(part, values))
        for part, (_, _, values) in zip(exps, problems)
    ]
    return peaks, totals, outs


def lanes_of(columns):
    _, j = grid_ij((columns[0].shape[0], 128))
    block = jnp.zeros((columns[0].shape[0], 128), FULL)
    for lane, column in enumerate(columns):
        block = jnp.where(j == lane, column, block)
    return block


def near_kernel(q_ref, *refs):
    k_refs, v_refs, (out_ref, stat_ref) = refs[:4], refs[4:8], refs[8:]
    parts = heads_of(0, 5)
    peaks, totals, outs = softmax_all(
        [(q_ref[:, c], [k[:, c] for k in k_refs], [v[:, c] for v in v_refs]) for _, c in parts]
    )
    for (_, c), out, total in zip(parts, outs, totals):
        out_ref[:, c] = out * (1.0 / total)
    block = lanes_of([peak + jnp.log2(total) for peak, total in zip(peaks, totals)])
    stat_ref[0] = block.T[0:8]


def joined(refs, rows, c):
    return jnp.concatenate([r[:, :, rows, c].reshape(256, HD) for r in refs], 0)


def group_rows(a_ref, b_ref, y_ref, c):
    one = {
        "k": a_ref[0, :, 0:32, c], "v": a_ref[0, :, 32:64, c],
        "q": b_ref[0, :, 0:32, c], "g": b_ref[0, :, 32:64, c],
    }
    one = {name: x.reshape(128, HD) for name, x in one.items()}
    two = {name: y_ref[0, t, 0:16, c] for t, name in enumerate("kvqg")}
    return one, two


def group_forward_kernel(zs_ref, *refs):
    a0, a1, (y0, y1, ret_ref) = refs[0:2], refs[2:4], refs[4:]
    problems = []
    parts = heads_of(0, 3)
    for _, c in parts:
        q1 = zs_ref[:, 80:112, c].reshape(128, HD)
        problems.append((
            q1,
            [joined(r, slice(0, 32), c) for r in (a0, a1)],
            [joined(r, slice(32, 64), c) for r in (a0, a1)],
        ))
        problems.append((
            y0[0, 2, 0:16, c],
            [y[:, 0, :, c].reshape(256, HD) for y in (y0, y1)],
            [y[:, 1, :, c].reshape(256, HD) for y in (y0, y1)],
        ))
    peaks, totals, outs = softmax_all(problems)
    outs = [out * (1.0 / total) for out, total in zip(outs, totals)]
    lses = [peak + jnp.log2(total) for peak, total in zip(peaks, totals)]
    one, two = lanes_of(lses[0::2]), lanes_of(lses[1::2])
    for m in range(4):
        for (_, c), out1, out2 in zip(parts, outs[0::2], outs[1::2]):
            ret_ref[m, 0:32, c] = out1[32 * m : 32 * m + 32]
            ret_ref[m, 32:36, c] = out2[4 * m : 4 * m + 4]
        ret_ref[m, 0:32, 384:512] = one[32 * m : 32 * m + 32]
        ret_ref[m, 32:36, 384:512] = two[4 * m : 4 * m + 4]
        ret_ref[m, 36:40, :] = jnp.zeros((4, 512), FULL)


def thirds_of(x):
    pieces = []
    for _ in range(3):
        pieces.append(x.astype(HALF))
        x = x - pieces[-1].astype(FULL)
    return pieces


def row_times(row, onehot):
    i, _ = grid_ij((8, row.shape[1]))
    rows = jnp.zeros((8, row.shape[1]), FULL)
    for n, piece in enumerate(thirds_of(row)):
        rows = jnp.where(i == n, piece.astype(FULL), rows)
    return jnp.sum(dot_nn(rows.astype(HALF), onehot), 0, keepdims=True)


def transposed(rows):
    rows = list(rows)
    width = rows[0].shape[1]
    return jnp.concatenate(rows + [jnp.zeros((128 - len(rows), width), FULL)], 0).T


def merge_kernel(
    off_ref, near_ref, near_stat_ref, g_ref, ret_ref, att_ref, stat_ref, row_ref, sel_ref
):
    lses, scales, picked, far_scales, hits = [], [], [], [], []
    for h in range(H):
        mine = h // 3
        i, p = grid_ij((40, ROWS))
        one = (i < 32) & (p == 8 * i + off_ref[1, h])
        two = (i >= 32) & (i < 36) & (p == 64 * (i - 32) + off_ref[2, h])
        far = ret_ref[mine, :, 384:512].T[h % 3 : h % 3 + 1]
        both = row_times(far, jnp.concatenate([one, two], 1).astype(HALF))
        _, p = grid_ij((1, ROWS))
        lse0 = near_stat_ref[h // 5, h % 5 : h % 5 + 1, :]
        lse1 = jnp.where((p & 7) == off_ref[1, h], both[:, :ROWS], NEG)
        lse2 = jnp.where((p & 63) == off_ref[2, h], both[:, ROWS:], NEG)
        peak = jnp.maximum(jnp.maximum(lse0, lse1), lse2)
        total = jnp.exp2(lse0 - peak) + jnp.exp2(lse1 - peak) + jnp.exp2(lse2 - peak)
        lses.append(peak + jnp.log2(total))
        scales.append(jnp.exp2(lse0 - lses[-1]))
        p, j = grid_ij((ROWS, 128))
        target = jnp.where(j < 32, 8 * j + off_ref[1, h], 64 * (j - 32) + off_ref[2, h])
        hits.append(((p == target) & (j < 36)).astype(HALF))
        picked.append(row_times(lses[-1], hits[-1]))
        _, j = grid_ij((1, 40))
        far_scale = jnp.where(j < 36, jnp.exp2(jnp.minimum(far - picked[-1][:, :40], 1.0)), 0.0)
        far_scales.append(jnp.concatenate([far_scale, jnp.zeros((1, 88), FULL)], 1))
    scales = transposed(scales)
    far_scales = transposed(far_scales)
    dots = []
    for h, c in heads_of(0, H):
        mine, lane = h // 3, slice(h % 3 * HD, (h % 3 + 1) * HD)
        far = ret_ref[mine, :, lane] * far_scales[:40, h : h + 1]
        high = far.astype(HALF)
        low = (far - high.astype(FULL)).astype(HALF)
        lifted = dot_nn(hits[h][:, :40], jnp.concatenate([high, low], 1))
        out = near_ref[:, c] * scales[:, h : h + 1] + lifted[:, :HD] + lifted[:, HD:]
        att_ref[:, c] = out.astype(HALF)
        dots.append(jnp.sum(out * g_ref[:, c].astype(FULL), 1, keepdims=True))
    dots = lanes_of(dots).T
    dots = [dots[h : h + 1] for h in range(H)]
    for s in range(2):
        stat_ref[s] = transposed(lses[5 * s : 5 * s + 5] + dots[5 * s : 5 * s + 5])
    for s in range(5):
        rows = lses[2 * s : 2 * s + 2] + dots[2 * s : 2 * s + 2]
        row_ref[s] = jnp.concatenate(rows + [jnp.zeros((4, ROWS), FULL)], 0)
    picked += [jnp.zeros((1, 128), FULL)] * 2
    dots = [row_times(dots[h], hits[h]) for h in range(H)] + [jnp.zeros((1, 128), FULL)] * 2
    packed = jnp.zeros((8, 128), FULL)
    for j in range(3):
        rows = jnp.concatenate(picked[j::3] + dots[j::3], 0)
        packed = packed + (pltpu.roll(rows, 40 * j, 1) if j else rows)
    for z in range(4):
        block = jnp.concatenate([packed[z : z + 1], packed[4 + z : 5 + z]], 0)
        for i in range(32):
            sel_ref[i // 8 * 32 + 8 * z + i % 8] = block


def gradients(problems):
    probs = [jnp.exp2(dot_nt(a, b) * FACTOR - lse) for a, b, _, _, lse, _ in problems]
    dprobs = [dot_nt(c, d) for _, _, c, d, _, _ in problems]
    return [
        (prob.astype(HALF), (prob * (dprob - row_dot)).astype(HALF))
        for prob, dprob, (_, _, _, _, _, row_dot) in zip(probs, dprobs, problems)
    ]


def near_query_kernel(q_ref, g_ref, stat_ref, *refs):
    k_refs, v_refs, (dq_ref,) = refs[:4], refs[4:8], refs[8:]
    problems = []
    for part, (_, c) in enumerate(heads_of(0, 5)):
        lse = stat_ref[0, :, part : part + 1]
        row_dot = stat_ref[0, :, part + 5 : part + 6]
        for k, v in zip(k_refs, v_refs):
            problems.append((q_ref[:, c], k[:, c], g_ref[:, c], v[:, c], lse, row_dot))
    done = gradients(problems)
    for part, (_, c) in enumerate(heads_of(0, 5)):
        dq = sum(dot_nn(ds, k[:, c]) for (_, ds), k in zip(done[4 * part :], k_refs))
        dq_ref[:, c] = dq.astype(HALF)


def gathered_stats(s_ref, c):
    _, lane = grid_ij((2, 128))
    one = [[], [], []]
    two = [[jnp.zeros((2, 128), FULL)] * 2 for _ in range(3)]

    def moved(rows, distance):
        return pltpu.roll(rows, distance % 128, 1) if distance % 128 else rows

    for y in range(4):
        for x, x_mask in enumerate(MASKS4):
            blocks = [jnp.zeros((2, 128), FULL)] * 3
            for z in range(4):
                source = (lax.axis_index("seqhi") ^ y) * 32 + (
                    8 * z + ((lax.axis_index("seqlo") & 7) ^ (2 * x_mask + c))
                )
                rows = s_ref[source]
                start = 64 * (y % 2) + 16 * x + 4 * z
                for j in range(3):
                    if y == 0:
                        blocks[j] = jnp.where(lane // 32 == z, moved(rows, 32 * z - 40 * j), blocks[j])
                    two[j][y // 2] = jnp.where(
                        (lane >= start) & (lane < start + 4),
                        moved(rows, start - 32 - 40 * j),
                        two[j][y // 2],
                    )
            if y == 0:
                for j in range(3):
                    one[j].append(blocks[j])
    return [jnp.concatenate(x, 1) for x in one], [jnp.concatenate(x, 1) for x in two]


def group_backward_kernel(*refs):
    a0, a1, b0, b1 = refs[0:2], refs[2:4], refs[4:6], refs[6:8]
    y0, y1, s_ref, out_ref = refs[8:]
    problems, others = [], []
    parts = heads_of(0, 3)
    s10, s20 = gathered_stats(s_ref, 0)
    s11, s21 = gathered_stats(s_ref, 1)
    for j, c in parts:
        one, two = group_rows(a0[0], b0[0], y0, c)
        sides = []
        for a, b, s in ((a0, b0, s10), (a1, b1, s11)):
            sides.append((
                joined(a, slice(0, 32), c), joined(a, slice(32, 64), c),
                joined(b, slice(0, 32), c), joined(b, slice(32, 64), c),
                s[j][0:1], s[j][1:2],
            ))
        for y, s in ((y0, s20), (y1, s21)):
            sides.append(
                tuple(y[:, t, :, c].reshape(256, HD) for t in range(4))
                + (s[j][0:1], s[j][1:2]))
        own = (one, one, two, two)
        for rows, n, (k, v, q, g, lse, row_dot) in zip(own, (128, 128, 16, 16), sides):
            first = sides[0] if n == 128 else sides[2]
            lse_own = eye_column(first[4][:, :n], n)
            dot_own = eye_column(first[5][:, :n], n)
            problems.append((rows["q"], k, rows["g"], v, lse_own, dot_own))
            others.append(k)
            problems.append((rows["k"], q, rows["v"], g, lse, row_dot))
            others.append((q, g))
    done = gradients(problems)
    for j, c in parts:
        mine, rest = done[8 * j : 8 * j + 8], others[8 * j : 8 * j + 8]
        dq = [dot_nn(mine[n][1], rest[n]) * SCALING for n in (0, 2, 4, 6)]
        dk = [dot_nn(mine[n][1], rest[n][0]) * SCALING for n in (1, 3, 5, 7)]
        dv = [dot_nn(mine[n][0], rest[n][1]) for n in (1, 3, 5, 7)]
        one = [(x[0] + x[1]).astype(HALF) for x in (dq, dk, dv)]
        two = [x[2] + x[3] for x in (dq, dk, dv)]
        for m in range(4):
            for t in range(3):
                out_ref[m, 32 * t : 32 * t + 32, c] = one[t][32 * m : 32 * m + 32]
            small = [x[4 * m : 4 * m + 4] for x in two] + [jnp.zeros((4, HD), FULL)]
            out_ref[m, 96:112, c] = jnp.concatenate(small, 0).astype(HALF)


def near_key_kernel(k_ref, v_ref, *refs):
    qg_refs, s_refs, (dk_ref, dv_ref) = refs[:4], refs[4:8], refs[8:]
    problems = []
    for part, (_, c) in enumerate(heads_of(0)):
        for qg, s in zip(qg_refs, s_refs):
            lse, row_dot = s[0, part : part + 1, :], s[0, part + 2 : part + 3, :]
            problems.append((k_ref[:, c], qg[0, :, c], v_ref[:, c], qg[1, :, c], lse, row_dot))
    done = gradients(problems)
    for part, (_, c) in enumerate(heads_of(0)):
        mine = done[4 * part : 4 * part + 4]
        dk = sum(dot_nn(ds, qg[0, :, c]) for (_, ds), qg in zip(mine, qg_refs))
        dk_ref[:, c] = dk.astype(HALF)
        dv = sum(dot_nn(prob, qg[1, :, c]) for (prob, _), qg in zip(mine, qg_refs))
        dv_ref[:, c] = dv.astype(HALF)


def add_kernel(
    off_ref, dq_near_ref, dk_near_ref, dv_near_ref, back_ref, dq_ref, dk_ref, dv_ref
):
    p, r = grid_ij((ROWS, 112))
    tensor = jnp.where(r < 96, r // 32, (r - 96) // 4)
    for h, c in heads_of(pl.program_id(0), 5):
        target = jnp.where(r < 96, 8 * (r & 31) + off_ref[1, h], 64 * (r & 3) + off_ref[2, h])
        hit = p == target
        rows = back_ref[h // 3, :, pl.ds(pl.multiple_of(h % 3 * HD, HD), HD)]
        lifted = [dot_nn((hit & (tensor == t)).astype(HALF), rows) for t in range(3)]
        dq_ref[:, c] = (dq_near_ref[:, c].astype(FULL) * SCALING + lifted[0]).astype(HALF)
        dk_ref[:, c] = (dk_near_ref[:, c].astype(FULL) * SCALING + lifted[1]).astype(HALF)
        dv_ref[:, c] = (dv_near_ref[:, c].astype(FULL) + lifted[2]).astype(HALF)


COLUMNS = pl.BlockSpec((ROWS, 2 * HD), lambda s, *_: (0, s))
PAIR = pl.BlockSpec((2, ROWS, 2 * HD), lambda s, *_: (0, 0, s))
FIVE = pl.BlockSpec((ROWS, 5 * HD), lambda s, *_: (0, s))
LANES = pl.BlockSpec((1, ROWS, 128), lambda s, *_: (s, 0, 0))
STAT_ROWS = pl.BlockSpec((1, 8, ROWS), lambda s, *_: (s, 0, 0))


def whole(*shape):
    return pl.BlockSpec(shape, lambda *_: (0,) * len(shape))


def array(*shape, dtype=HALF):
    return jax.ShapeDtypeStruct(shape, dtype)


def call(kernel, name, steps, in_specs, out_specs, out_shape, operands, prefetch=0, room=60, time=0.001):
    return pl.pallas_call(
        kernel,
        grid_spec=pltpu.PrefetchScalarGridSpec(
            num_scalar_prefetch=prefetch, grid=(steps,), in_specs=in_specs, out_specs=out_specs
        ),
        out_shape=out_shape,
        compiler_params=pltpu.CompilerParams(vmem_limit_bytes=room * 1024 * 1024),
        cost_estimate=pl.CostEstimate(flops=int(time * 1_150_000_000), bytes_accessed=100_000, transcendentals=0),
        name=name,
    )(*operands)


CORE, X1, X3 = 1, 2, 6
MASKS4 = (0, 1, 3, 2)
ZS = (8, 16, 24)


def two_steps(x, axis, first, second):
    x = jnp.stack([x, swapped(x, axis, first)])
    return jnp.concatenate([x, swapped(x, axis, second)], 0)


def around(x, axis, masks):
    return [x] + [swapped(x, axis, m) for m in masks]


def over_z(parts):
    groups = [[8 * z + i for z in range(4)] for i in range(8)]
    return lax.all_to_all(parts, "seqlo", 0, 0, axis_index_groups=groups, tiled=True)


def core(x):
    return swapped(x, "seqlo", CORE)


def body(query, key, value, grad_out, offsets):
    kx = swapped(key, "seqlo", X1)
    zs = call(
        pick_kernel, "pick_rows", 1, [whole(*WIDE)] * 4, [whole(4, 144, 384)],
        [array(4, 144, 384)], (offsets, key, value, query, grad_out), prefetch=1,
    )[0]
    zs = over_z(zs)
    a, y, b, kx = together(zs[:, :64], zs[:, 64:80], zs[:, 80:], kx)
    y = jnp.stack([y, swapped(y, "seqlo", X1)])
    a, y, b = together(a, y, b)
    a, b = [jnp.stack([t, swapped(t, "seqlo", X1)]) for t in (a, b)]
    y = jnp.concatenate([y, swapped(y, "seqlo", X3)], 0)
    value_out, a, b, y = together(value, a, b, y)
    vx = swapped(value_out, "seqlo", X1)
    a3 = swapped(a, "seqlo", X3)
    y = y.reshape(4, 4, 4, 4, 384).transpose(2, 0, 1, 3, 4).reshape(4, 64, 384)
    y = around(y, "seqhi", (1, 2, 3))
    a3, *y = together(a3, *y)
    b3 = swapped(b, "seqlo", X3)
    both, vx = together(jnp.stack([query, grad_out]), vx)
    both_x = swapped(both, "seqlo", X1)
    y = jnp.stack(y)
    a, y = [a, a3, core(a), core(a3)], [y, core(y)]
    part_spec, y_spec = whole(2, 4, 64, 384), whole(4, 4, 64, 384)
    (ret,) = call(
        group_forward_kernel, "group_forward", 1,
        [whole(4, 144, 384)] + [part_spec] * 4 + [y_spec] * 2, [whole(4, 40, 512)],
        [array(4, 40, 512, dtype=FULL)], (zs, *a, *y),
    )
    near_query, ret = together(query, ret)
    ret = over_z(ret)
    keys0 = [key, core(key), kx, core(kx)]
    values0 = [value, core(value), vx, core(vx)]
    near, near_stat = call(
        near_kernel, "near_forward", 2, [FIVE] * 9, [FIVE, STAT_ROWS],
        [array(*WIDE, dtype=FULL), array(2, 8, ROWS, dtype=FULL)],
        (near_query, *keys0, *values0),
    )
    ret, near_stat, b3 = together(ret, near_stat, b3)
    attended, stat, rows, sel = call(
        merge_kernel, "merge_levels", 1,
        [whole(*WIDE), whole(2, 8, ROWS), whole(*WIDE), whole(4, 40, 512)],
        [whole(*WIDE), whole(2, ROWS, 128), whole(5, 8, ROWS), whole(128, 2, 128)],
        [
            array(*WIDE), array(2, ROWS, 128, dtype=FULL), array(5, 8, ROWS, dtype=FULL),
            array(128, 2, 128, dtype=FULL),
        ],
        (offsets, near, near_stat, grad_out, ret), prefetch=1,
    )

    sel = lax.all_to_all(sel, ("seqhi", "seqlo"), 0, 0, tiled=True)
    b = [b, b3, core(b), core(b3)]
    sx = swapped(rows, "seqlo", X1)
    stat, both_x = together(stat, both_x)
    both = [both, core(both), both_x, core(both_x)]
    (dq_near,) = call(
        near_query_kernel, "near_query_gradient", 2, [FIVE] * 2 + [LANES] + [FIVE] * 8,
        [FIVE], [array(*WIDE)],
        (query, grad_out, stat, *keys0, *values0), time=8,
    )
    sel, sx, dq_near = together(sel, sx, dq_near)
    (back,) = call(
        group_backward_kernel, "group_backward", 1,
        [part_spec] * 8 + [y_spec] * 2 + [whole(128, 2, 128)],
        [whole(4, 112, 384)], [array(4, 112, 384)],
        (*a, *b, *y, sel),
    )
    s0 = [rows, core(rows), sx, core(sx)]
    s0[0], back = together(rows, back)
    dk_near, dv_near = call(
        near_key_kernel, "near_key_gradient", 5, [COLUMNS] * 2 + [PAIR] * 4 + [STAT_ROWS] * 4, [COLUMNS] * 2,
        [array(*WIDE)] * 2, (key, value, *both, *s0),
    )
    back = over_z(back)
    back, dk_near = together(back, dk_near)
    grad_query, grad_key, grad_value = call(
        add_kernel, "add_levels", 2,
        [FIVE] * 3 + [whole(4, 112, 384)], [FIVE] * 3, [array(*WIDE)] * 3,
        (offsets, dq_near, dk_near, dv_near, back), prefetch=1,
    )
    return attended, grad_query, grad_key, grad_value


def solution(mesh):
    spec = P(("seqhi", "seqlo"), None)
    return jax.shard_map(
        body,
        mesh=mesh,
        in_specs=(spec, spec, spec, spec, P()),
        out_specs=(spec, spec, spec, spec),
        check_vma=False,
    )
```
